512 devices in a mesh: gx: 32 (over y, x, z_hi), gy: 16 (over z_lo, core).
Axes of the slice: x: 4, y: 4, z: 16 (z_hi: 2, z_lo: 8; z = z_hi * 8 + z_lo), core: 2. Of those that a mesh axis runs over, the one named last changes fastest.
Arguments:
- points: bfloat16 [131072, 2048], P(('gx', 'gy')), may hold values from -8 to 8
- residual: float32 [131072, 1000], P(('gx', 'gy')), may hold values from -6 to 6
- block_ids: int32 [512], replicated, may hold values from 0 to 131071, as said below
Outputs:
- updated: float32 [131072, 1000], P(('gx', 'gy'))
- block_step: float32 [512, 1000], P('gy')
The draws below stay inside these ranges and needn't reach their ends.
Inputs may be any that keep to these rules, and one draw needn't show every extreme that they name: `block_ids`: the 512 indices are distinct. The 256 consecutive indices of one device hold at most 2 of them, and some device holds exactly 2. The 16 devices of one gx index, 4096 consecutive indices, hold at most 24, and some such group holds exactly 24.
All inputs are finite; a program needn't handle non-finite values.
Results may differ from the reference program's by a relative error of at most 0.0003.
Values may be sent and summed in bfloat16 or wider, within the bound.
No kernel may reach another device: no remote copies, remote signals or barrier semaphores. Data moves between devices by JAX's collectives and lax.ppermute only.
A program may use at most 64 MiB of HBM per device.

```python
import jax
import jax.numpy as jnp
from jax import lax

D = 2048
C = 1000
BLK = 512
PTS_DEV = 256
TOTAL = 131072
CAP = 2
N_GX = 32
N_GY = 16


def draw_points(key, part):
    key = jax.random.fold_in(key, 11)
    base_key, order_key, rough_key = jax.random.split(key, 3)
    ranking = jax.random.permutation(order_key, D).astype(jnp.float32)
    column_scale = lax.rsqrt(1.0 + ranking) * jnp.exp(jax.random.uniform(rough_key, (D,), jnp.float32, -0.35, 0.35))
    values = jnp.clip(jax.random.normal(base_key, (TOTAL, D), jnp.float32), -5.0, 5.0)
    return (values * column_scale[None, :]).astype(jnp.bfloat16)


def shuffle_slots(subkey):
    return jax.random.permutation(subkey, N_GY * CAP)


def shuffle_rows(subkey):
    return jax.random.permutation(subkey, PTS_DEV)


def draw_block_ids(key, part):
    key = jax.random.fold_in(key, 23)
    key_list = jax.random.split(key, 7)
    pair_count = N_GX // 2
    group_mean = BLK // N_GX
    spread = group_mean // 2
    amount = jax.random.randint(key_list[0], (pair_count,), 0, spread + 1)
    forced_pair = jax.random.randint(key_list[1], (), 0, pair_count)
    amount = jnp.where(jnp.arange(pair_count) == forced_pair, spread, amount)
    loads = jnp.stack([group_mean + amount, group_mean - amount], axis=1).reshape(N_GX)
    loads = loads[jax.random.permutation(key_list[2], N_GX)]
    slot_count = N_GY * CAP
    forced_device = jax.random.randint(key_list[3], (N_GX,), 0, N_GY)
    device_in_group = jnp.arange(slot_count, dtype=jnp.int32) // CAP
    shuffled = jax.vmap(shuffle_slots)(jax.random.split(key_list[4], N_GX))
    priority = jnp.where(device_in_group[None, :] == forced_device[:, None], 0, slot_count)
    order_rank = jnp.argsort(jnp.argsort(priority + shuffled, axis=1), axis=1)
    taken = order_rank < loads[:, None]
    row_choice = jax.vmap(shuffle_rows)(jax.random.split(key_list[5], N_GX * N_GY))[:, :CAP]
    device_flat = jnp.arange(N_GX, dtype=jnp.int32)[:, None] * N_GY + device_in_group[None, :]
    slot_in_device = jnp.arange(slot_count, dtype=jnp.int32) % CAP
    picked_rows = row_choice[device_flat, jnp.broadcast_to(slot_in_device[None, :], device_flat.shape)]
    candidates = (device_flat * PTS_DEV + picked_rows).reshape(N_GX * slot_count)
    mixing = jax.random.permutation(key_list[6], N_GX * slot_count)
    ordering = jnp.where(taken.reshape(N_GX * slot_count), 0, N_GX * slot_count) + mixing
    chosen = jnp.argsort(ordering)[:BLK]
    return candidates[chosen].astype(jnp.int32)


def shard_levels(key, dims, cuts, smallest, top_value):
    gain, own = 1.0, jax.random.fold_in(key, 6)
    for position, blocks in cuts:
        steps = jnp.exp(jax.random.uniform(jax.random.fold_in(own, position), (blocks,), jnp.float32, smallest / len(cuts), top_value / len(cuts)))
        gain = gain * jnp.repeat(steps, dims[position] // blocks).reshape([-1 if axis == position else 1 for axis in range(len(dims))])
    return gain


def bell_draw(own_key, shape, scale, bound, shards=(), kind=jnp.bfloat16):
    drawn = scale * jax.random.normal(own_key, shape, jnp.float32)
    if shards:
        drawn = drawn * shard_levels(own_key, shape, shards, -0.22, 0.18)
    return jnp.clip(drawn, -bound, bound).astype(kind)


def setup_inputs(seed: int = 0) -> dict:
    splits = jax.random.split(jax.random.key(seed), 4)
    points = draw_points(jax.random.fold_in(splits[3], 71), 0)
    residual = bell_draw(splits[1], (TOTAL, C), 1.0, 6.0, ((0, 512),), jnp.float32)
    block_ids = draw_block_ids(jax.random.fold_in(splits[3], 71), 0)
    return dict(points=points, residual=residual, block_ids=block_ids)


GAMMA = 0.125
RIDGE = 0.5

def kernel(left, right):
    left_sq = jnp.sum(jnp.square(left.astype(jnp.float32)), axis=1)
    right_sq = jnp.sum(jnp.square(right.astype(jnp.float32)), axis=1)
    cross = lax.dot_general(left.astype(jnp.float32), right.astype(jnp.float32), (((1,), (1,)), ((), ())), preferred_element_type=jnp.float32)
    return jnp.exp(-GAMMA * (left_sq[:, None] + right_sq[None, :] - 2.0 * cross))

def reference(points, residual, block_ids):
    block_points = jnp.take(points, block_ids, axis=0)
    block_resid = jnp.take(residual, block_ids, axis=0)
    gram = kernel(block_points, block_points) + RIDGE * jnp.eye(BLK, dtype=jnp.float32)
    factor = jnp.linalg.cholesky(gram)
    block_step = jax.scipy.linalg.cho_solve((factor, True), block_resid)

    def update(pieces):
        point_rows, resid_rows = pieces
        return resid_rows - jnp.dot(kernel(point_rows, block_points), block_step, precision=lax.Precision.HIGHEST)
    updated = lax.map(update, (points.reshape(TOTAL // PTS_DEV, PTS_DEV, D), residual.reshape(TOTAL // PTS_DEV, PTS_DEV, C)))
    updated = updated.reshape(TOTAL, C)
    updated = updated.at[block_ids].add(-RIDGE * block_step)
    return (updated, block_step)
```

```python
import functools

import jax
import jax.numpy as jnp
from jax import lax
from jax.experimental import pallas as pl
from jax.experimental.pallas import tpu as pltpu
from jax.sharding import Mesh
from jax.sharding import PartitionSpec as P

F32=jnp.float32; BF=jnp.bfloat16
NN=(((1,),(0,)),((),())); NT=(((1,),(1,)),((),()))
def dot(a,b,dn=NN,prec=None):
    return lax.dot_general(a,b,dn,preferred_element_type=F32,precision=prec)
def split(v):
    hi=v.astype(BF); return hi,(v-hi.astype(F32)).astype(BF)
def mm3(a,b):
    ah,al=a; bh,bl=b
    return dot(ah,bh)+(dot(ah,bl)+dot(al,bh))
HI=lax.Precision.HIGHEST
def factor_body(info, idrow, own_ref, oth_ref, pts_ref, w_ref, g_ref, gh_ref, gl_ref, x_ref, m_ref, *, half, share):
    n=own_ref.shape[0]; rows=pts_ref.shape[0]
    core=info[0]; first=info[1]; share0=info[2]
    own=own_ref[...]; oth=oth_ref[...]
    cross=dot(own,own,NT)+dot(oth,oth,NT)
    ri=lax.broadcasted_iota(jnp.int32,(n,n),0); ci=lax.broadcasted_iota(jnp.int32,(n,n),1)
    eye=ri==ci
    diag=jnp.where(eye,cross,0.0)
    sq_row=jnp.sum(diag,axis=0,keepdims=True); sq_col=jnp.sum(diag,axis=1,keepdims=True)
    gram=jnp.exp(-0.125*(sq_col+sq_row-2.0*cross))+jnp.where(eye,0.5,0.0)
    g_ref[...]=gram
    gh,gl=split(gram); gh_ref[...]=gh; gl_ref[...]=gl
    p_own=pts_ref[:,pl.ds(pl.multiple_of(core*half,half),half)]
    p_oth=pts_ref[:,pl.ds(pl.multiple_of((1-core)*half,half),half)]
    pf=pts_ref[...].astype(F32)
    psq=jnp.sum(pf*pf,axis=1,keepdims=True)
    pc=dot(p_own,own,NT)+dot(p_oth,oth,NT)
    pk=jnp.exp(-0.125*(psq+sq_row-2.0*pc))
    pid=first+lax.broadcasted_iota(jnp.int32,(rows,n),0)
    m_ref[pl.ds(0,rows),:]=pk+jnp.where(pid==idrow[...],0.5,0.0)
    sid=share0+lax.broadcasted_iota(jnp.int32,(share,n),0)
    m_ref[pl.ds(rows,share),:]=jnp.where(sid==lax.broadcasted_iota(jnp.int32,(share,n),1),1.0,0.0)
    lo=0.499; hi=jnp.max(jnp.sum(gram,axis=0,keepdims=True))*1.001
    s=2.0/(lo+hi)
    x_ref[...]=jnp.where(eye,2.0*s,0.0)-(s*s)*gram
    d=(hi-lo)/(hi+lo)
    def cond(resid): return resid>1e-4
    def body(resid):
        s=2.0/(2.0-resid)
        x=x_ref[...]*s
        xs=split(x)
        t=mm3((gh_ref[...],gl_ref[...]),xs)
        r=jnp.where(eye,1.0,0.0)-t
        x_ref[...]=x+mm3(xs,split(r))
        dn=resid/(2.0-resid)
        return dn*dn
    lax.while_loop(cond,body,d*d)
    m=m_ref[...]
    xs=split(x_ref[...])
    w=mm3(split(m),xs)
    e=m-dot(w,g_ref[...],NN,HI)
    w_ref[...]=w+mm3(split(e),xs)
def factor(info,ids,own,oth,pts,share):
    n=own.shape[0]; rows=pts.shape[0]
    V=pl.BlockSpec(memory_space=pltpu.VMEM)
    return pl.pallas_call(functools.partial(factor_body,half=own.shape[1],share=share),
        out_shape=jax.ShapeDtypeStruct((rows+share,n),F32),
        in_specs=[pl.BlockSpec(memory_space=pltpu.SMEM),V,V,V,V],out_specs=V,
        scratch_shapes=[pltpu.VMEM((n,n),F32),pltpu.VMEM((n,n),BF),pltpu.VMEM((n,n),BF),pltpu.VMEM((n,n),F32),pltpu.VMEM((rows+share,n),F32)],
        compiler_params=pltpu.CompilerParams(vmem_limit_bytes=48*1024*1024),
    )(info,ids.reshape(1,n),own,oth,pts)


PLANE = ("y", "x")
COLUMN = ("zh", "zl", "c")
EVERY = PLANE + COLUMN
CAP = 2
COL_CAP = 48
CLASS_PAD = 1024


def three_parts(value):
    hi = lax.reduce_precision(value, 8, 7)
    mid = lax.reduce_precision(value - hi, 8, 7)
    low = lax.reduce_precision((value - hi) - mid, 8, 7)
    return hi.astype(BF), mid.astype(BF), low.astype(BF)


def on_device(points, residual, block_ids):
    rows, feats = points.shape
    classes = residual.shape[1]
    block = block_ids.shape[0]
    n_plane = lax.axis_size(PLANE)
    n_col = lax.axis_size(COLUMN)
    plane = lax.axis_index(PLANE)
    place = lax.axis_index(COLUMN)
    core = lax.axis_index("c")
    me = plane * n_col + place
    half = feats // 2
    chalf = CLASS_PAD // 2

    owner = block_ids // rows
    column = block_ids // (rows * n_col)
    less = block_ids[:, None] > block_ids[None, :]
    slot = jnp.sum(jnp.where(less & (owner[:, None] == owner[None, :]), 1, 0), axis=1).astype(jnp.int32)
    rank = jnp.sum(jnp.where(less & (column[:, None] == column[None, :]), 1, 0), axis=1).astype(jnp.int32)
    mine = owner == me
    picked_points, picked_resid = [], []
    for k in range(CAP):
        row = jnp.sum(jnp.where(mine & (slot == k), block_ids - me * rows, 0)).astype(jnp.int32)
        picked_points.append(lax.dynamic_slice(points, (row, 0), (1, feats)))
        picked_resid.append(lax.dynamic_slice(residual, (row, 0), (1, classes)))
    my_points = jnp.concatenate(picked_points, axis=0)
    my_resid = jnp.pad(jnp.concatenate(picked_resid, axis=0), ((0, 0), (0, CLASS_PAD - classes)))
    hi, mid, low = three_parts(my_resid)
    parts = [my_points.reshape(CAP, 2, half)] + [v.reshape(CAP, 2, chalf) for v in (hi, mid, low)]
    packed = jnp.concatenate(parts, axis=2).transpose(1, 0, 2)
    width = packed.shape[2]
    packed = jnp.broadcast_to(packed[None], (n_col // 2, 2, CAP, width)).reshape(n_col, CAP, width)
    column_rows = lax.all_to_all(packed, COLUMN, 0, 0, tiled=True).reshape(n_col * CAP, width)

    in_column = column == plane
    sel_rank = in_column[None, :] & (rank[None, :] == jnp.arange(COL_CAP, dtype=jnp.int32)[:, None])
    col_slot = (owner % n_col) * CAP + slot
    sel_slot = col_slot[:, None] == jnp.arange(n_col * CAP, dtype=jnp.int32)[None, :]
    pick = dot(sel_rank.astype(BF), sel_slot.astype(BF)).astype(BF)
    compact = dot(pick, column_rows).astype(BF)
    col_points = compact[:, :half]
    r_hi, r_mid, r_low = [compact[:, half + k * chalf : half + (k + 1) * chalf].astype(F32) for k in range(3)]
    col_resid = (r_hi + r_mid) + r_low

    resid_own = lax.all_gather(col_resid, PLANE, axis=0, tiled=True)
    spread = jnp.broadcast_to(col_points[None], (n_plane, COL_CAP, half))
    plane_rows = lax.all_to_all(spread, PLANE, 0, 0, tiled=True).reshape(n_plane * COL_CAP, half)
    place_of = (column * COL_CAP + rank)[:, None] == jnp.arange(n_plane * COL_CAP, dtype=jnp.int32)[None, :]
    place_of = place_of.astype(BF)
    own = dot(place_of, plane_rows).astype(BF)
    other = lax.ppermute(own, "c", [(0, 1), (1, 0)])

    share = block // (lax.axis_size("zl") * lax.axis_size("c"))
    share_at = (place % (lax.axis_size("zl") * lax.axis_size("c"))) * share
    info = jnp.stack([core, me * rows, share_at]).astype(jnp.int32)
    weights = factor(info, block_ids, own, other, points, share)
    w_hi, w_mid, w_low = three_parts(weights)
    spread_w = (dot(w_hi, place_of) + dot(w_mid, place_of)) + dot(w_low, place_of)

    resid_other = lax.ppermute(resid_own, "c", [(0, 1), (1, 0)])
    first = core == 0
    resid = jnp.concatenate([jnp.where(first, resid_own, resid_other), jnp.where(first, resid_other, resid_own)], axis=1)
    change = dot(spread_w, resid[:, :classes], prec=HI)
    return (residual - change[:rows], change[rows:])


def solution(mesh):
    fine = Mesh(mesh.devices.reshape(4, 4, 2, 8, 2), EVERY)
    return jax.shard_map(
        on_device,
        mesh=fine,
        in_specs=(P(EVERY, None), P(EVERY, None), P()),
        out_specs=(P(EVERY, None), P(("zl", "c"), None)),
        check_vma=False,
    )
```

```python
import functools

import jax
import jax.numpy as jnp
from jax import lax
from jax.experimental import pallas as pl
from jax.experimental.pallas import tpu as pltpu
from jax.sharding import Mesh
from jax.sharding import PartitionSpec as P

F32 = jnp.float32
BF = jnp.bfloat16
I32 = jnp.int32
HI = lax.Precision.HIGHEST
NN = (((1,), (0,)), ((), ()))
NT = (((1,), (1,)), ((), ()))
TN = (((0,), (0,)), ((), ()))

GAMMA = 0.125
RIDGE = 0.5
PLANE = ("y", "x")
COLUMN = ("zh", "zl", "c")
EVERY = PLANE + COLUMN
CAP = 2
COL_CAP = 48
CLASS_PAD = 1024
SPLIT = 4
MIB = 1024 * 1024


def dot(a, b, dn=NN, prec=None):
    return lax.dot_general(a, b, dn, preferred_element_type=F32, precision=prec)


def iota(shape, axis):
    return lax.broadcasted_iota(I32, shape, axis)


def two_parts(v):
    hi = v.astype(BF)
    return hi, (v - hi.astype(F32)).astype(BF)


def mm3(a, b):
    ah, al = a
    bh, bl = b
    return dot(ah, bh) + (dot(ah, bl) + dot(al, bh))


def vmem():
    return pl.BlockSpec(memory_space=pltpu.VMEM)


def smem():
    return pl.BlockSpec(memory_space=pltpu.SMEM)


def params(mib):
    return pltpu.CompilerParams(vmem_limit_bytes=mib * MIB)


def pack_body(info, ids_ref, pts_ref, res_ref, out_ref, rank_ref, slot_ref, *, n_col):
    me = info[2]
    rows = pts_ref.shape[0]
    ids = ids_ref[...]
    n = ids.shape[1]
    eye = iota((n, n), 0) == iota((n, n), 1)
    ids_col = jnp.sum(jnp.where(eye, jnp.broadcast_to(ids, (n, n)), 0), axis=1, keepdims=True)
    owner = ids // rows
    column = ids // (rows * n_col)
    less = jnp.broadcast_to(ids_col, (n, n)) < ids
    rank = jnp.sum(jnp.where(less & (ids_col >= column * (rows * n_col)), 1, 0), axis=0, keepdims=True)
    slot = jnp.sum(jnp.where(less & (ids_col >= owner * rows), 1, 0), axis=0, keepdims=True)
    rank_ref[...] = rank
    slot_ref[...] = slot
    mine = owner == me
    lane = iota((8, rows), 1)
    sub = iota((8, rows), 0)
    take = jnp.zeros((8, rows), F32)
    for k in range(CAP):
        at = jnp.max(jnp.where(mine & (slot == k), ids - me * rows, -1), axis=1, keepdims=True)
        take = jnp.where((sub == k) & (lane == at), 1.0, take)
    take = take.astype(BF)
    picked = dot(take, pts_ref[...]).astype(BF)
    res = res_ref[...]
    hi = res.astype(BF)
    rest = res - hi.astype(F32)
    mid = rest.astype(BF)
    low = (rest - mid.astype(F32)).astype(BF)
    classes = res.shape[0]
    pad = jnp.zeros((8, CLASS_PAD - classes), F32)
    parts = [jnp.concatenate([dot(take, v, NT), pad], axis=1).astype(BF) for v in (hi, mid, low)]
    half = pts_ref.shape[1] // 2
    chalf = CLASS_PAD // 2
    for core in range(2):
        row = [picked[:CAP, core * half : (core + 1) * half]]
        row += [v[:CAP, core * chalf : (core + 1) * chalf] for v in parts]
        row = jnp.concatenate(row, axis=1).astype(F32)
        w = row.shape[1] // SPLIT
        block = jnp.concatenate([row[:, q * w : (q + 1) * w] for q in range(SPLIT)], axis=0).astype(BF)
        for z in range(n_col // 2):
            out_ref[2 * z + core] = block


def pack(info, ids, points, res_t, n_col):
    width = points.shape[1] // 2 + 3 * CLASS_PAD // 2
    n = ids.shape[1]
    return pl.pallas_call(
        functools.partial(pack_body, n_col=n_col),
        out_shape=(
            jax.ShapeDtypeStruct((n_col, CAP * SPLIT, width // SPLIT), BF),
            jax.ShapeDtypeStruct((1, n), I32),
            jax.ShapeDtypeStruct((1, n), I32),
        ),
        in_specs=[smem(), vmem(), vmem(), vmem()],
        out_specs=(vmem(), vmem(), vmem()),
        compiler_params=params(32),
    )(info, ids, points, res_t)


def compact_body(info, ids_ref, rank_ref, slot_ref, in_ref, pts_ref, res_ref, *, rows, n_col):
    plane = info[1]
    ids = ids_ref[...]
    n = ids.shape[1]
    owner = ids // rows
    column = ids // (rows * n_col)
    wide = in_ref.shape[0]
    sel_rank = (iota((COL_CAP, n), 0) == rank_ref[...]) & (column == plane)
    at = iota((wide, n), 0)
    group = CAP * SPLIT
    sel_slot = (at // group == owner - column * n_col) & (at % CAP == slot_ref[...])
    pick = dot(sel_rank.astype(F32).astype(BF), sel_slot.astype(F32).astype(BF), NT)
    part = (iota((COL_CAP, wide), 1) // CAP) % SPLIT
    data = in_ref[...]
    whole = [dot(jnp.where(part == q, pick, 0.0).astype(BF), data) for q in range(SPLIT)]
    whole = jnp.concatenate(whole, axis=1)
    half = pts_ref.shape[2]
    chalf = CLASS_PAD // 2
    pts = whole[:, :half].astype(BF)
    res = whole[:, half : half + chalf] + whole[:, half + chalf : half + 2 * chalf]
    res = res + whole[:, half + 2 * chalf :]
    for p in range(pts_ref.shape[0]):
        pts_ref[p] = pts
        res_ref[p] = res


def compact(info, ids, rank, slot, data, rows, half, n_plane, n_col):
    return pl.pallas_call(
        functools.partial(compact_body, rows=rows, n_col=n_col),
        out_shape=(
            jax.ShapeDtypeStruct((n_plane, COL_CAP, half), BF),
            jax.ShapeDtypeStruct((n_plane, COL_CAP, CLASS_PAD // 2), F32),
        ),
        in_specs=[smem(), vmem(), vmem(), vmem(), vmem()],
        out_specs=(vmem(), vmem()),
        compiler_params=params(32),
    )(info, ids, rank, slot, data)


def place_matrix(ids, rank, wide, span):
    return (iota((wide, ids.shape[1]), 0) == (ids // span) * COL_CAP + rank).astype(F32).astype(BF)


def order_body(ids_ref, rank_ref, in_ref, out_ref, *, span):
    place = place_matrix(ids_ref[...], rank_ref[...], in_ref.shape[0], span)
    out_ref[...] = dot(place, in_ref[...], TN).astype(BF)


def order(ids, rank, data, span):
    return pl.pallas_call(
        functools.partial(order_body, span=span),
        out_shape=jax.ShapeDtypeStruct((ids.shape[1], data.shape[1]), BF),
        in_specs=[vmem(), vmem(), vmem()],
        out_specs=vmem(),
        compiler_params=params(32),
    )(ids, rank, data)


def weights_body(info, ids_ref, rank_ref, own_ref, oth_ref, pts_ref, hi_ref, lo_ref, g_ref, gh_ref, gl_ref, x_ref, m_ref, *, half, share, span):
    n = own_ref.shape[0]
    rows = pts_ref.shape[0]
    core, me, share_at = info[0], info[2], info[3]
    own = own_ref[...]
    oth = oth_ref[...]
    cross = dot(own, own, NT) + dot(oth, oth, NT)
    eye = iota((n, n), 0) == iota((n, n), 1)
    diag = jnp.where(eye, cross, 0.0)
    sq_row = jnp.sum(diag, axis=0, keepdims=True)
    sq_col = jnp.sum(diag, axis=1, keepdims=True)
    gram = jnp.exp(-GAMMA * (sq_col + sq_row - 2.0 * cross)) + jnp.where(eye, RIDGE, 0.0)
    g_ref[...] = gram
    gh, gl = two_parts(gram)
    gh_ref[...] = gh
    gl_ref[...] = gl
    p_own = pts_ref[:, pl.ds(pl.multiple_of(core * half, half), half)]
    p_oth = pts_ref[:, pl.ds(pl.multiple_of((1 - core) * half, half), half)]
    pf = pts_ref[...].astype(F32)
    psq = jnp.sum(pf * pf, axis=1, keepdims=True)
    p_cross = dot(p_own, own, NT) + dot(p_oth, oth, NT)
    p_kern = jnp.exp(-GAMMA * (psq + sq_row - 2.0 * p_cross))
    point_id = me * rows + iota((rows, n), 0)
    m_ref[pl.ds(0, rows), :] = p_kern + jnp.where(point_id == ids_ref[...], RIDGE, 0.0)
    m_ref[pl.ds(rows, share), :] = jnp.where(share_at + iota((share, n), 0) == iota((share, n), 1), 1.0, 0.0)
    lo = 0.499
    hi = jnp.max(jnp.sum(gram, axis=0, keepdims=True)) * 1.001
    s = 2.0 / (lo + hi)
    x_ref[...] = jnp.where(eye, 2.0 * s, 0.0) - (s * s) * gram
    d = (hi - lo) / (hi + lo)

    def refine(resid):
        x = x_ref[...] * (2.0 / (2.0 - resid))
        xs = two_parts(x)
        r = jnp.where(eye, 1.0, 0.0) - mm3((gh_ref[...], gl_ref[...]), xs)
        x_ref[...] = x + mm3(xs, two_parts(r))
        after = resid / (2.0 - resid)
        return after * after

    lax.while_loop(lambda resid: resid > 1e-4, refine, d * d)
    m = m_ref[...]
    xs = two_parts(x_ref[...])
    w = mm3(two_parts(m), xs)
    e = m - dot(w, g_ref[...], NN, HI)
    w = w + mm3(two_parts(e), xs)
    place = place_matrix(ids_ref[...], rank_ref[...], hi_ref.shape[1], span)
    wh, wl = two_parts(w)
    hi_ref[...] = dot(wh, place, NT).astype(BF)
    lo_ref[...] = dot(wl, place, NT).astype(BF)


def weights(info, ids, rank, own, oth, points, share, wide, span):
    n = own.shape[0]
    rows = points.shape[0]
    out = jax.ShapeDtypeStruct((rows + share, wide), BF)
    return pl.pallas_call(
        functools.partial(weights_body, half=own.shape[1], share=share, span=span),
        out_shape=(out, out),
        in_specs=[smem()] + [vmem()] * 5,
        out_specs=(vmem(), vmem()),
        scratch_shapes=[
            pltpu.VMEM((n, n), F32),
            pltpu.VMEM((n, n), BF),
            pltpu.VMEM((n, n), BF),
            pltpu.VMEM((n, n), F32),
            pltpu.VMEM((rows + share, n), F32),
        ],
        compiler_params=params(48),
        cost_estimate=pl.CostEstimate(flops=10**10, bytes_accessed=6 * 10**6, transcendentals=4 * 10**5),
    )(info, ids, rank, own, oth, points)


def update_body(info, hi_ref, lo_ref, own_ref, oth_ref, res_ref, out_ref, share_ref, ch_ref):
    core = info[0]
    rows = res_ref.shape[1]
    classes = res_ref.shape[0]
    chalf = own_ref.shape[1]
    w = hi_ref[...], lo_ref[...]
    ch_ref[:, pl.ds(pl.multiple_of(core * chalf, chalf), chalf)] = mm3(w, two_parts(own_ref[...]))
    ch_ref[:, pl.ds(pl.multiple_of((1 - core) * chalf, chalf), chalf)] = mm3(w, two_parts(oth_ref[...]))
    share_ref[...] = ch_ref[pl.ds(rows, share_ref.shape[0]), pl.ds(0, classes)]
    out_ref[...] = res_ref[...] - ch_ref[pl.ds(0, rows), :].T[:classes]


def update(info, hi, lo, own, oth, res_t, share):
    classes, rows = res_t.shape
    return pl.pallas_call(
        update_body,
        out_shape=(jax.ShapeDtypeStruct((classes, rows), F32), jax.ShapeDtypeStruct((share, classes), F32)),
        in_specs=[smem()] + [vmem()] * 5,
        out_specs=(vmem(), vmem()),
        scratch_shapes=[pltpu.VMEM((rows + share, CLASS_PAD), F32)],
        compiler_params=params(48),
    )(info, hi, lo, own, oth, res_t)


def on_device(points, residual, block_ids):
    rows, feats = points.shape
    block = block_ids.shape[0]
    n_plane = lax.axis_size(PLANE)
    n_col = lax.axis_size(COLUMN)
    n_gy = lax.axis_size("zl") * lax.axis_size("c")
    plane = lax.axis_index(PLANE)
    place = lax.axis_index(COLUMN)
    share = block // n_gy
    half = feats // 2
    wide = n_plane * COL_CAP
    span = rows * n_col
    info = jnp.stack([lax.axis_index("c"), plane, plane * n_col + place, (place % n_gy) * share]).astype(I32)
    ids = block_ids.reshape(1, block)
    res_t = residual.T
    swap = [(0, 1), (1, 0)]

    packed, rank, slot = pack(info, ids, points, res_t, n_col)
    col_rows = lax.all_to_all(packed, COLUMN, 0, 0, tiled=True)
    col_rows = col_rows.reshape(n_col * CAP * SPLIT, col_rows.shape[2])
    pts_out, res_out = compact(info, ids, rank, slot, col_rows, rows, half, n_plane, n_col)
    all_pts = lax.all_to_all(pts_out, PLANE, 0, 0, tiled=True).reshape(wide, half)
    all_res = lax.all_to_all(res_out, PLANE, 0, 0, tiled=True).reshape(wide, CLASS_PAD // 2)
    own = order(ids, rank, all_pts, span)
    other = lax.ppermute(own, "c", swap)
    hi, lo = weights(info, ids, rank, own, other, points, share, wide, span)
    other_res = lax.ppermute(all_res, "c", swap)
    out_t, step_share = update(info, hi, lo, all_res, other_res, res_t, share)
    return (out_t.T, step_share)


def solution(mesh):
    fine = Mesh(mesh.devices.reshape(4, 4, 2, 8, 2), EVERY)
    return jax.shard_map(
        on_device,
        mesh=fine,
        in_specs=(P(EVERY, None), P(EVERY, None), P()),
        out_specs=(P(EVERY, None), P(("zl", "c"), None)),
        check_vma=False,
    )
```

```python
import functools

import jax
import jax.numpy as jnp
from jax import lax
from jax.experimental import pallas as pl
from jax.experimental.pallas import tpu as pltpu
from jax.sharding import Mesh
from jax.sharding import PartitionSpec as P

F32 = jnp.float32
BF = jnp.bfloat16
I32 = jnp.int32
HI = lax.Precision.HIGHEST
NN = (((1,), (0,)), ((), ()))
NT = (((1,), (1,)), ((), ()))
TN = (((0,), (0,)), ((), ()))

GAMMA = 0.125
RIDGE = 0.5
PLANE = ("y", "x")
COLUMN = ("zh", "zl", "c")
EVERY = PLANE + COLUMN
CAP = 2
COL_CAP = 48
CLASS_PAD = 1024
SPLIT = 4
MIB = 1024 * 1024


def dot(a, b, dn=NN, prec=None):
    return lax.dot_general(a, b, dn, preferred_element_type=F32, precision=prec)


def iota(shape, axis):
    return lax.broadcasted_iota(I32, shape, axis)


def two_parts(v):
    hi = v.astype(BF)
    return hi, (v - hi.astype(F32)).astype(BF)


def mm3(a, b):
    ah, al = a
    bh, bl = b
    return dot(ah, bh) + (dot(ah, bl) + dot(al, bh))


def vmem():
    return pl.BlockSpec(memory_space=pltpu.VMEM)


def smem():
    return pl.BlockSpec(memory_space=pltpu.SMEM)


def hbm():
    return pl.BlockSpec(memory_space=pltpu.HBM)


def params(mib):
    return pltpu.CompilerParams(vmem_limit_bytes=mib * MIB)


def pack_body(info, ids_hbm, pts_hbm, res_hbm, out_ref, tab_ref, ids_ref, pts_ref, res_ref, sems, *, n_col):
    me = info[2]
    rows = pts_ref.shape[0]
    ids_in = pltpu.make_async_copy(ids_hbm, ids_ref, sems.at[0])
    pts_in = pltpu.make_async_copy(pts_hbm, pts_ref, sems.at[1])
    res_in = pltpu.make_async_copy(res_hbm, res_ref, sems.at[2])
    ids_in.start()
    pts_in.start()
    res_in.start()
    ids_in.wait()
    ids = ids_ref[...]
    n = ids.shape[1]
    eye = iota((n, n), 0) == iota((n, n), 1)
    ids_col = jnp.sum(jnp.where(eye, jnp.broadcast_to(ids, (n, n)), 0), axis=1, keepdims=True)
    owner = ids // rows
    column = ids // (rows * n_col)
    less = jnp.broadcast_to(ids_col, (n, n)) < ids
    rank = jnp.sum(jnp.where(less & (ids_col >= column * (rows * n_col)), 1, 0), axis=0, keepdims=True)
    slot = jnp.sum(jnp.where(less & (ids_col >= owner * rows), 1, 0), axis=0, keepdims=True)
    tab_ref[...] = jnp.concatenate([ids, rank, slot, jnp.zeros((5, n), I32)], axis=0)
    mine = owner == me
    lane = iota((8, rows), 1)
    sub = iota((8, rows), 0)
    take = jnp.zeros((8, rows), F32)
    for k in range(CAP):
        at = jnp.max(jnp.where(mine & (slot == k), ids - me * rows, -1), axis=1, keepdims=True)
        take = jnp.where((sub == k) & (lane == at), 1.0, take)
    take = take.astype(BF)
    pts_in.wait()
    picked = dot(take, pts_ref[...]).astype(BF)
    res_in.wait()
    res = res_ref[...]
    hi = res.astype(BF)
    rest = res - hi.astype(F32)
    mid = rest.astype(BF)
    low = (rest - mid.astype(F32)).astype(BF)
    classes = res.shape[0]
    pad = jnp.zeros((8, CLASS_PAD - classes), F32)
    parts = [jnp.concatenate([dot(take, v, NT), pad], axis=1).astype(BF) for v in (hi, mid, low)]
    half = pts_ref.shape[1] // 2
    chalf = CLASS_PAD // 2
    for core in range(2):
        row = [picked[:CAP, core * half : (core + 1) * half]]
        row += [v[:CAP, core * chalf : (core + 1) * chalf] for v in parts]
        row = jnp.concatenate(row, axis=1).astype(F32)
        w = row.shape[1] // SPLIT
        block = jnp.concatenate([row[:, q * w : (q + 1) * w] for q in range(SPLIT)], axis=0).astype(BF)
        for z in range(n_col // 2):
            out_ref[2 * z + core] = block


def pack(info, ids, points, res_t, n_col):
    width = points.shape[1] // 2 + 3 * CLASS_PAD // 2
    n = ids.shape[1]
    return pl.pallas_call(
        functools.partial(pack_body, n_col=n_col),
        out_shape=(
            jax.ShapeDtypeStruct((n_col, CAP * SPLIT, width // SPLIT), BF),
            jax.ShapeDtypeStruct((8, n), I32),
        ),
        in_specs=[smem(), hbm(), hbm(), hbm()],
        out_specs=(vmem(), vmem()),
        scratch_shapes=[
            pltpu.VMEM(ids.shape, I32),
            pltpu.VMEM(points.shape, BF),
            pltpu.VMEM(res_t.shape, F32),
            pltpu.SemaphoreType.DMA((3,)),
        ],
        compiler_params=params(60),
    )(info, ids, points, res_t)


def table(tab_ref):
    return tab_ref[0:1, :], tab_ref[1:2, :], tab_ref[2:3, :]


def compact_body(info, tab_ref, in_ref, pts_ref, res_ref, *, rows, n_col):
    plane = info[1]
    ids, rank, slot = table(tab_ref)
    n = ids.shape[1]
    owner = ids // rows
    column = ids // (rows * n_col)
    wide = in_ref.shape[0]
    sel_rank = (iota((COL_CAP, n), 0) == rank) & (column == plane)
    at = iota((wide, n), 0)
    group = CAP * SPLIT
    sel_slot = (at // group == owner - column * n_col) & (at % CAP == slot)
    pick = dot(sel_rank.astype(F32).astype(BF), sel_slot.astype(F32).astype(BF), NT)
    part = (iota((COL_CAP, wide), 1) // CAP) % SPLIT
    data = in_ref[...]
    whole = [dot(jnp.where(part == q, pick, 0.0).astype(BF), data) for q in range(SPLIT)]
    whole = jnp.concatenate(whole, axis=1)
    half = pts_ref.shape[2]
    chalf = CLASS_PAD // 2
    pts = whole[:, :half].astype(BF)
    res = whole[:, half : half + chalf] + whole[:, half + chalf : half + 2 * chalf]
    res = res + whole[:, half + 2 * chalf :]
    for p in range(pts_ref.shape[0]):
        pts_ref[p] = pts
        res_ref[p] = res


def compact(info, tab, data, rows, half, n_plane, n_col):
    return pl.pallas_call(
        functools.partial(compact_body, rows=rows, n_col=n_col),
        out_shape=(
            jax.ShapeDtypeStruct((n_plane, COL_CAP, half), BF),
            jax.ShapeDtypeStruct((n_plane, COL_CAP, CLASS_PAD // 2), F32),
        ),
        in_specs=[smem(), vmem(), vmem()],
        out_specs=(vmem(), vmem()),
        compiler_params=params(16),
    )(info, tab, data)


def place_matrix(tab_ref, wide, span):
    ids, rank, _ = table(tab_ref)
    return (iota((wide, ids.shape[1]), 0) == (ids // span) * COL_CAP + rank).astype(F32).astype(BF)


def order_body(tab_ref, in_ref, out_ref, *, span):
    out_ref[...] = dot(place_matrix(tab_ref, in_ref.shape[0], span), in_ref[...], TN).astype(BF)


def order(tab, data, span):
    return pl.pallas_call(
        functools.partial(order_body, span=span),
        out_shape=jax.ShapeDtypeStruct((tab.shape[1], data.shape[1]), BF),
        in_specs=[vmem(), vmem()],
        out_specs=vmem(),
        compiler_params=params(10),
    )(tab, data)


def first_half_body(info, pts_ref, own_ref, cross_ref, p_cross_ref, psq_ref, p_oth_ref, *, half):
    core = info[0]
    own = own_ref[...]
    cross_ref[...] = dot(own, own, NT)
    p_own = pts_ref[:, pl.ds(pl.multiple_of(core * half, half), half)]
    p_oth = pts_ref[:, pl.ds(pl.multiple_of((1 - core) * half, half), half)]
    p_cross_ref[...] = dot(p_own, own, NT)
    p_oth_ref[...] = p_oth
    a = p_own.astype(F32)
    b = p_oth.astype(F32)
    psq_ref[...] = jnp.sum(a * a, axis=1, keepdims=True) + jnp.sum(b * b, axis=1, keepdims=True)


def first_half(info, points, own):
    n, half = own.shape
    rows = points.shape[0]
    return pl.pallas_call(
        functools.partial(first_half_body, half=half),
        out_shape=(
            jax.ShapeDtypeStruct((n, n), F32),
            jax.ShapeDtypeStruct((rows, n), F32),
            jax.ShapeDtypeStruct((rows, 1), F32),
            jax.ShapeDtypeStruct((rows, half), BF),
        ),
        in_specs=[smem(), vmem(), vmem()],
        out_specs=(vmem(),) * 4,
        compiler_params=params(12),
        cost_estimate=pl.CostEstimate(flops=2 * 10**9, bytes_accessed=3 * 10**6, transcendentals=0),
    )(info, points, own)


def inverse_body(info, tab_ref, p_oth_ref, oth_ref, cross_ref, p_cross_ref, psq_ref, hi_ref, lo_ref, g_ref, m_ref, gh_ref, gl_ref, x_ref, *, share):
    n = oth_ref.shape[0]
    rows = p_cross_ref.shape[0]
    me, share_at = info[2], info[3]
    oth = oth_ref[...]
    cross = cross_ref[...] + dot(oth, oth, NT)
    eye = iota((n, n), 0) == iota((n, n), 1)
    diag = jnp.where(eye, cross, 0.0)
    sq_row = jnp.sum(diag, axis=0, keepdims=True)
    sq_col = jnp.sum(diag, axis=1, keepdims=True)
    gram = jnp.exp(-GAMMA * (sq_col + sq_row - 2.0 * cross)) + jnp.where(eye, RIDGE, 0.0)
    g_ref[...] = gram
    gh, gl = two_parts(gram)
    gh_ref[...] = gh
    gl_ref[...] = gl
    p_cross = p_cross_ref[...] + dot(p_oth_ref[...], oth, NT)
    p_kern = jnp.exp(-GAMMA * (psq_ref[...] + sq_row - 2.0 * p_cross))
    point_id = me * rows + iota((rows, n), 0)
    m_ref[pl.ds(0, rows), :] = p_kern + jnp.where(point_id == table(tab_ref)[0], RIDGE, 0.0)
    m_ref[pl.ds(rows, share), :] = jnp.where(share_at + iota((share, n), 0) == iota((share, n), 1), 1.0, 0.0)
    lo = 0.499
    gram = g_ref[...]
    v_col = jnp.sum(gram, axis=1, keepdims=True)
    v_row = jnp.sum(gram, axis=0, keepdims=True)
    hi = jnp.max(jnp.sum(gram * v_col, axis=0, keepdims=True) / v_row) * 1.001
    s = 2.0 / (lo + hi)
    x_ref[...] = jnp.where(eye, 2.0 * s, 0.0) - (s * s) * gram
    d = (hi - lo) / (hi + lo)

    def refine(resid):
        x = x_ref[...] * (2.0 / (2.0 - resid))
        xh, xl = two_parts(x)
        r = (jnp.where(eye, 1.0, 0.0) - mm3((gh_ref[...], gl_ref[...]), (xh, xl))).astype(BF)
        x_ref[...] = x + (dot(xh, r) + dot(xl, r))
        after = resid / (2.0 - resid)
        return after * after

    lax.while_loop(lambda resid: resid > 5e-4, refine, d * d)
    xs = two_parts(x_ref[...])
    m = m_ref[...]
    w = mm3(two_parts(m), xs)
    e = m - dot(w, g_ref[...], NN, HI)
    w = w + mm3(two_parts(e), xs)
    wh, wl = two_parts(w)
    hi_ref[...] = wh
    lo_ref[...] = wl


def inverse(info, tab, p_oth, oth, cross, p_cross, psq, share):
    n = oth.shape[0]
    rows = p_oth.shape[0]
    out = jax.ShapeDtypeStruct((rows + share, n), BF)
    return pl.pallas_call(
        functools.partial(inverse_body, share=share),
        out_shape=(out, out),
        in_specs=[smem()] + [vmem()] * 6,
        out_specs=(vmem(), vmem()),
        scratch_shapes=[
            pltpu.VMEM((n, n), F32),
            pltpu.VMEM((rows + share, n), F32),
            pltpu.VMEM((n, n), BF),
            pltpu.VMEM((n, n), BF),
            pltpu.VMEM((n, n), F32),
        ],
        compiler_params=params(18),
        cost_estimate=pl.CostEstimate(flops=12 * 10**9, bytes_accessed=6 * 10**6, transcendentals=4 * 10**5),
    )(info, tab, p_oth, oth, cross, p_cross, psq)


def update_own_body(tab_ref, wh_ref, wl_ref, res_ref, hi_ref, lo_ref, ch_ref, *, span):
    place = place_matrix(tab_ref, res_ref.shape[0], span)
    hi = dot(wh_ref[...], place, NT).astype(BF)
    lo = dot(wl_ref[...], place, NT).astype(BF)
    hi_ref[...] = hi
    lo_ref[...] = lo
    ch_ref[...] = mm3((hi, lo), two_parts(res_ref[...]))


def update_own(tab, wh, wl, res, span):
    m = wh.shape[0]
    wide, chalf = res.shape
    out = jax.ShapeDtypeStruct((m, wide), BF)
    return pl.pallas_call(
        functools.partial(update_own_body, span=span),
        out_shape=(out, out, jax.ShapeDtypeStruct((m, chalf), F32)),
        in_specs=[vmem()] * 4,
        out_specs=(vmem(),) * 3,
        compiler_params=params(10),
        cost_estimate=pl.CostEstimate(flops=2 * 10**9, bytes_accessed=4 * 10**6, transcendentals=0),
    )(tab, wh, wl, res)


def update_other_body(info, hi_ref, lo_ref, res_ref, ch_ref, res_t_ref, out_ref, share_ref, all_ref):
    core = info[0]
    classes, rows = res_t_ref.shape
    chalf = res_ref.shape[1]
    all_ref[:, pl.ds(pl.multiple_of(core * chalf, chalf), chalf)] = ch_ref[...]
    change = mm3((hi_ref[...], lo_ref[...]), two_parts(res_ref[...]))
    all_ref[:, pl.ds(pl.multiple_of((1 - core) * chalf, chalf), chalf)] = change
    share_ref[...] = all_ref[pl.ds(rows, share_ref.shape[0]), pl.ds(0, classes)]
    out_ref[...] = res_t_ref[...] - all_ref[pl.ds(0, rows), :].T[:classes]


def update_other(info, hi, lo, res, change, res_t, share):
    classes, rows = res_t.shape
    return pl.pallas_call(
        update_other_body,
        out_shape=(jax.ShapeDtypeStruct((classes, rows), F32), jax.ShapeDtypeStruct((share, classes), F32)),
        in_specs=[smem()] + [vmem()] * 5,
        out_specs=(vmem(), vmem()),
        scratch_shapes=[pltpu.VMEM((rows + share, CLASS_PAD), F32)],
        compiler_params=params(16),
    )(info, hi, lo, res, change, res_t)


def on_device(points, residual, block_ids):
    rows, feats = points.shape
    block = block_ids.shape[0]
    n_plane = lax.axis_size(PLANE)
    n_col = lax.axis_size(COLUMN)
    n_gy = lax.axis_size("zl") * lax.axis_size("c")
    plane = lax.axis_index(PLANE)
    place = lax.axis_index(COLUMN)
    share = block // n_gy
    half = feats // 2
    wide = n_plane * COL_CAP
    span = rows * n_col
    info = jnp.stack([lax.axis_index("c"), plane, plane * n_col + place, (place % n_gy) * share]).astype(I32)
    ids = block_ids.reshape(1, block)
    res_t = residual.T
    swap = [(0, 1), (1, 0)]

    packed, tab = pack(info, ids, points, res_t, n_col)
    col_rows = lax.all_to_all(packed, COLUMN, 0, 0, tiled=True)
    col_rows = col_rows.reshape(n_col * CAP * SPLIT, col_rows.shape[2])
    pts_out, res_out = compact(info, tab, col_rows, rows, half, n_plane, n_col)
    all_pts = lax.all_to_all(pts_out, PLANE, 0, 0, tiled=True).reshape(wide, half)
    all_res = lax.all_to_all(res_out, PLANE, 0, 0, tiled=True).reshape(wide, CLASS_PAD // 2)
    own = order(tab, all_pts, span)
    other = lax.ppermute(own, "c", swap)
    cross, p_cross, psq, p_oth = first_half(info, points, own)
    wh, wl = inverse(info, tab, p_oth, other, cross, p_cross, psq, share)
    all_res, wh = lax.optimization_barrier((all_res, wh))
    other_res = lax.ppermute(all_res, "c", swap)
    hi, lo, change = update_own(tab, wh, wl, all_res, span)
    out_t, step_share = update_other(info, hi, lo, other_res, change, res_t, share)
    return (out_t.T, step_share)


def solution(mesh):
    fine = Mesh(mesh.devices.reshape(4, 4, 2, 8, 2), EVERY)
    return jax.shard_map(
        on_device,
        mesh=fine,
        in_specs=(P(EVERY, None), P(EVERY, None), P()),
        out_specs=(P(EVERY, None), P(("zl", "c"), None)),
        check_vma=False,
    )
```

```python
import functools

import jax
import jax.numpy as jnp
from jax import lax
from jax.experimental import pallas as pl
from jax.experimental.pallas import tpu as pltpu
from jax.sharding import Mesh
from jax.sharding import PartitionSpec as P

F32 = jnp.float32
BF = jnp.bfloat16
I32 = jnp.int32
HI = lax.Precision.HIGHEST
NN = (((1,), (0,)), ((), ()))
NT = (((1,), (1,)), ((), ()))
TN = (((0,), (0,)), ((), ()))

GAMMA = 0.125
RIDGE = 0.5
PLANE = ("y", "x")
COLUMN = ("zh", "zl", "c")
EVERY = PLANE + COLUMN
CAP = 2
COL_CAP = 48
CLASS_PAD = 1024
SPLIT = 4
MIB = 1024 * 1024


def dot(a, b, dn=NN, prec=None):
    return lax.dot_general(a, b, dn, preferred_element_type=F32, precision=prec)


def iota(shape, axis):
    return lax.broadcasted_iota(I32, shape, axis)


def two_parts(v):
    hi = v.astype(BF)
    return hi, (v - hi.astype(F32)).astype(BF)


def mm3(a, b):
    ah, al = a
    bh, bl = b
    return dot(ah, bh) + (dot(ah, bl) + dot(al, bh))


def vmem():
    return pl.BlockSpec(memory_space=pltpu.VMEM)


def smem():
    return pl.BlockSpec(memory_space=pltpu.SMEM)


def hbm():
    return pl.BlockSpec(memory_space=pltpu.HBM)


def params(mib):
    return pltpu.CompilerParams(vmem_limit_bytes=mib * MIB)


def pack_body(info, ids_hbm, pts_hbm, res_hbm, out_ref, tab_ref, ids_ref, pts_ref, res_ref, sems, *, n_col):
    me = info[2]
    rows = pts_ref.shape[0]
    ids_in = pltpu.make_async_copy(ids_hbm, ids_ref, sems.at[0])
    pts_in = pltpu.make_async_copy(pts_hbm, pts_ref, sems.at[1])
    res_in = pltpu.make_async_copy(res_hbm, res_ref, sems.at[2])
    ids_in.start()
    pts_in.start()
    res_in.start()
    ids_in.wait()
    ids = ids_ref[...]
    n = ids.shape[1]
    eye = iota((n, n), 0) == iota((n, n), 1)
    ids_col = jnp.sum(jnp.where(eye, jnp.broadcast_to(ids, (n, n)), 0), axis=1, keepdims=True)
    owner = ids // rows
    column = ids // (rows * n_col)
    less = jnp.broadcast_to(ids_col, (n, n)) < ids
    rank = jnp.sum(jnp.where(less & (ids_col >= column * (rows * n_col)), 1, 0), axis=0, keepdims=True)
    slot = jnp.sum(jnp.where(less & (ids_col >= owner * rows), 1, 0), axis=0, keepdims=True)
    tab_ref[...] = jnp.concatenate([ids, rank, slot, jnp.zeros((5, n), I32)], axis=0)
    mine = owner == me
    lane = iota((8, rows), 1)
    sub = iota((8, rows), 0)
    take = jnp.zeros((8, rows), F32)
    for k in range(CAP):
        at = jnp.max(jnp.where(mine & (slot == k), ids - me * rows, -1), axis=1, keepdims=True)
        take = jnp.where((sub == k) & (lane == at), 1.0, take)
    take = take.astype(BF)
    pts_in.wait()
    picked = dot(take, pts_ref[...]).astype(BF)
    res_in.wait()
    res = res_ref[...]
    hi = res.astype(BF)
    low = (res - hi.astype(F32)).astype(BF)
    classes = res.shape[0]
    pad = jnp.zeros((8, CLASS_PAD - classes), F32)
    parts = [jnp.concatenate([dot(take, v, NT), pad], axis=1).astype(BF) for v in (hi, low)]
    half = pts_ref.shape[1] // 2
    chalf = CLASS_PAD // 2
    for core in range(2):
        row = [picked[:CAP, core * half : (core + 1) * half]]
        row += [v[:CAP, core * chalf : (core + 1) * chalf] for v in parts]
        row = jnp.concatenate(row, axis=1).astype(F32)
        w = row.shape[1] // SPLIT
        block = jnp.concatenate([row[:, q * w : (q + 1) * w] for q in range(SPLIT)], axis=0).astype(BF)
        for z in range(n_col // 2):
            out_ref[2 * z + core] = block


def pack(info, ids, points, res_t, n_col):
    width = points.shape[1] // 2 + CLASS_PAD
    n = ids.shape[1]
    return pl.pallas_call(
        functools.partial(pack_body, n_col=n_col),
        out_shape=(
            jax.ShapeDtypeStruct((n_col, CAP * SPLIT, width // SPLIT), BF),
            jax.ShapeDtypeStruct((8, n), I32),
        ),
        in_specs=[smem(), hbm(), hbm(), hbm()],
        out_specs=(vmem(), vmem()),
        scratch_shapes=[
            pltpu.VMEM(ids.shape, I32),
            pltpu.VMEM(points.shape, BF),
            pltpu.VMEM(res_t.shape, F32),
            pltpu.SemaphoreType.DMA((3,)),
        ],
        compiler_params=params(60),
    )(info, ids, points, res_t)


def table(tab_ref):
    return tab_ref[0:1, :], tab_ref[1:2, :], tab_ref[2:3, :]


def compact_body(info, tab_ref, in_ref, pts_ref, res_ref, *, rows, n_col):
    plane = info[1]
    ids, rank, slot = table(tab_ref)
    n = ids.shape[1]
    owner = ids // rows
    column = ids // (rows * n_col)
    wide = in_ref.shape[0]
    sel_rank = (iota((COL_CAP, n), 0) == rank) & (column == plane)
    at = iota((wide, n), 0)
    group = CAP * SPLIT
    sel_slot = (at // group == owner - column * n_col) & (at % CAP == slot)
    pick = dot(sel_rank.astype(F32).astype(BF), sel_slot.astype(F32).astype(BF), NT)
    part = (iota((COL_CAP, wide), 1) // CAP) % SPLIT
    data = in_ref[...]
    whole = [dot(jnp.where(part == q, pick, 0.0).astype(BF), data) for q in range(SPLIT)]
    whole = jnp.concatenate(whole, axis=1)
    half = pts_ref.shape[2]
    pts = whole[:, :half].astype(BF)
    res = whole[:, half:].astype(BF)
    for p in range(pts_ref.shape[0]):
        pts_ref[p] = pts
        res_ref[p] = res


def compact(info, tab, data, rows, half, n_plane, n_col):
    return pl.pallas_call(
        functools.partial(compact_body, rows=rows, n_col=n_col),
        out_shape=(
            jax.ShapeDtypeStruct((n_plane, COL_CAP, half), BF),
            jax.ShapeDtypeStruct((n_plane, COL_CAP, CLASS_PAD), BF),
        ),
        in_specs=[smem(), vmem(), vmem()],
        out_specs=(vmem(), vmem()),
        compiler_params=params(16),
    )(info, tab, data)


def place_matrix(tab_ref, wide, span):
    ids, rank, _ = table(tab_ref)
    return (iota((wide, ids.shape[1]), 0) == (ids // span) * COL_CAP + rank).astype(F32).astype(BF)


def order_body(tab_ref, in_ref, out_ref, *, span):
    out_ref[...] = dot(place_matrix(tab_ref, in_ref.shape[0], span), in_ref[...], TN).astype(BF)


def order(tab, data, span):
    return pl.pallas_call(
        functools.partial(order_body, span=span),
        out_shape=jax.ShapeDtypeStruct((tab.shape[1], data.shape[1]), BF),
        in_specs=[vmem(), vmem()],
        out_specs=vmem(),
        compiler_params=params(10),
    )(tab, data)


def first_half_body(info, pts_ref, own_ref, cross_ref, p_cross_ref, psq_ref, p_oth_ref, *, half):
    core = info[0]
    own = own_ref[...]
    cross_ref[...] = dot(own, own, NT)
    p_own = pts_ref[:, pl.ds(pl.multiple_of(core * half, half), half)]
    p_oth = pts_ref[:, pl.ds(pl.multiple_of((1 - core) * half, half), half)]
    p_cross_ref[...] = dot(p_own, own, NT)
    p_oth_ref[...] = p_oth
    a = p_own.astype(F32)
    b = p_oth.astype(F32)
    psq_ref[...] = jnp.sum(a * a, axis=1, keepdims=True) + jnp.sum(b * b, axis=1, keepdims=True)


def first_half(info, points, own):
    n, half = own.shape
    rows = points.shape[0]
    return pl.pallas_call(
        functools.partial(first_half_body, half=half),
        out_shape=(
            jax.ShapeDtypeStruct((n, n), F32),
            jax.ShapeDtypeStruct((rows, n), F32),
            jax.ShapeDtypeStruct((rows, 1), F32),
            jax.ShapeDtypeStruct((rows, half), BF),
        ),
        in_specs=[smem(), vmem(), vmem()],
        out_specs=(vmem(),) * 4,
        compiler_params=params(12),
        cost_estimate=pl.CostEstimate(flops=10**6, bytes_accessed=10**6, transcendentals=0),
    )(info, points, own)


def inverse_body(info, tab_ref, p_oth_ref, oth_ref, cross_ref, p_cross_ref, psq_ref, hi_ref, lo_ref, g_ref, m_ref, gh_ref, gl_ref, x_ref, *, share):
    n = oth_ref.shape[0]
    rows = p_cross_ref.shape[0]
    me, share_at = info[2], info[3]
    oth = oth_ref[...]
    cross = cross_ref[...] + dot(oth, oth, NT)
    eye = iota((n, n), 0) == iota((n, n), 1)
    diag = jnp.where(eye, cross, 0.0)
    sq_row = jnp.sum(diag, axis=0, keepdims=True)
    sq_col = jnp.sum(diag, axis=1, keepdims=True)
    gram = jnp.exp(-GAMMA * (sq_col + sq_row - 2.0 * cross)) + jnp.where(eye, RIDGE, 0.0)
    g_ref[...] = gram
    gh, gl = two_parts(gram)
    gh_ref[...] = gh
    gl_ref[...] = gl
    p_cross = p_cross_ref[...] + dot(p_oth_ref[...], oth, NT)
    p_kern = jnp.exp(-GAMMA * (psq_ref[...] + sq_row - 2.0 * p_cross))
    point_id = me * rows + iota((rows, n), 0)
    m_ref[pl.ds(0, rows), :] = p_kern + jnp.where(point_id == table(tab_ref)[0], RIDGE, 0.0)
    m_ref[pl.ds(rows, share), :] = jnp.where(share_at + iota((share, n), 0) == iota((share, n), 1), 1.0, 0.0)
    lo = 0.499
    gram = g_ref[...]
    v_col = jnp.sum(gram, axis=1, keepdims=True)
    v_row = jnp.sum(gram, axis=0, keepdims=True)
    hi = jnp.max(jnp.sum(gram * v_col, axis=0, keepdims=True) / v_row) * 1.001
    s = 2.0 / (lo + hi)
    x_ref[...] = jnp.where(eye, 2.0 * s, 0.0) - (s * s) * gram
    d = (hi - lo) / (hi + lo)

    def refine(resid):
        x = x_ref[...] * (2.0 / (2.0 - resid))
        xh, xl = two_parts(x)
        r = (jnp.where(eye, 1.0, 0.0) - mm3((gh_ref[...], gl_ref[...]), (xh, xl))).astype(BF)
        x_ref[...] = x + (dot(xh, r) + dot(xl, r))
        after = resid / (2.0 - resid)
        return after * after

    lax.while_loop(lambda resid: resid > 5e-4, refine, d * d)
    xs = two_parts(x_ref[...])
    m = m_ref[...]
    w = mm3(two_parts(m), xs)
    e = m - dot(w, g_ref[...], NN, HI)
    w = w + mm3(two_parts(e), xs)
    wh, wl = two_parts(w)
    hi_ref[...] = wh
    lo_ref[...] = wl


def inverse(info, tab, p_oth, oth, cross, p_cross, psq, share):
    n = oth.shape[0]
    rows = p_oth.shape[0]
    out = jax.ShapeDtypeStruct((rows + share, n), BF)
    return pl.pallas_call(
        functools.partial(inverse_body, share=share),
        out_shape=(out, out),
        in_specs=[smem()] + [vmem()] * 6,
        out_specs=(vmem(), vmem()),
        scratch_shapes=[
            pltpu.VMEM((n, n), F32),
            pltpu.VMEM((rows + share, n), F32),
            pltpu.VMEM((n, n), BF),
            pltpu.VMEM((n, n), BF),
            pltpu.VMEM((n, n), F32),
        ],
        compiler_params=params(18),
        cost_estimate=pl.CostEstimate(flops=10**6, bytes_accessed=10**6, transcendentals=0),
    )(info, tab, p_oth, oth, cross, p_cross, psq)


def apply_weights(hi, lo, res_ref):
    chalf = res_ref.shape[1] // 2
    return mm3((hi, lo), (res_ref[:, :chalf], res_ref[:, chalf:]))


def update_own_body(tab_ref, wh_ref, wl_ref, res_ref, hi_ref, lo_ref, ch_ref, *, span):
    place = place_matrix(tab_ref, res_ref.shape[0], span)
    hi = dot(wh_ref[...], place, NT).astype(BF)
    lo = dot(wl_ref[...], place, NT).astype(BF)
    hi_ref[...] = hi
    lo_ref[...] = lo
    ch_ref[...] = apply_weights(hi, lo, res_ref)


def update_own(tab, wh, wl, res, span):
    m = wh.shape[0]
    wide, parts = res.shape
    out = jax.ShapeDtypeStruct((m, wide), BF)
    return pl.pallas_call(
        functools.partial(update_own_body, span=span),
        out_shape=(out, out, jax.ShapeDtypeStruct((m, parts // 2), F32)),
        in_specs=[vmem()] * 4,
        out_specs=(vmem(),) * 3,
        compiler_params=params(10),
        cost_estimate=pl.CostEstimate(flops=2 * 10**9, bytes_accessed=4 * 10**6, transcendentals=0),
    )(tab, wh, wl, res)


def update_other_body(info, hi_ref, lo_ref, res_ref, ch_ref, res_t_ref, out_ref, share_ref, all_ref):
    core = info[0]
    classes, rows = res_t_ref.shape
    chalf = ch_ref.shape[1]
    all_ref[:, pl.ds(pl.multiple_of(core * chalf, chalf), chalf)] = ch_ref[...]
    change = apply_weights(hi_ref[...], lo_ref[...], res_ref)
    all_ref[:, pl.ds(pl.multiple_of((1 - core) * chalf, chalf), chalf)] = change
    share_ref[...] = all_ref[pl.ds(rows, share_ref.shape[0]), pl.ds(0, classes)]
    out_ref[...] = res_t_ref[...] - all_ref[pl.ds(0, rows), :].T[:classes]


def update_other(info, hi, lo, res, change, res_t, share):
    classes, rows = res_t.shape
    return pl.pallas_call(
        update_other_body,
        out_shape=(jax.ShapeDtypeStruct((classes, rows), F32), jax.ShapeDtypeStruct((share, classes), F32)),
        in_specs=[smem()] + [vmem()] * 5,
        out_specs=(vmem(), vmem()),
        scratch_shapes=[pltpu.VMEM((rows + share, CLASS_PAD), F32)],
        compiler_params=params(16),
    )(info, hi, lo, res, change, res_t)


def on_device(points, residual, block_ids):
    rows, feats = points.shape
    block = block_ids.shape[0]
    n_plane = lax.axis_size(PLANE)
    n_col = lax.axis_size(COLUMN)
    n_gy = lax.axis_size("zl") * lax.axis_size("c")
    plane = lax.axis_index(PLANE)
    place = lax.axis_index(COLUMN)
    share = block // n_gy
    half = feats // 2
    wide = n_plane * COL_CAP
    span = rows * n_col
    info = jnp.stack([lax.axis_index("c"), plane, plane * n_col + place, (place % n_gy) * share]).astype(I32)
    ids = block_ids.reshape(1, block)
    res_t = residual.T
    swap = [(0, 1), (1, 0)]

    packed, tab = pack(info, ids, points, res_t, n_col)
    col_rows = lax.all_to_all(packed, COLUMN, 0, 0, tiled=True)
    col_rows = col_rows.reshape(n_col * CAP * SPLIT, col_rows.shape[2])
    pts_out, res_out = compact(info, tab, col_rows, rows, half, n_plane, n_col)
    all_pts = lax.all_to_all(pts_out, PLANE, 0, 0, tiled=True).reshape(wide, half)
    all_res = lax.all_to_all(res_out, PLANE, 0, 0, tiled=True).reshape(wide, CLASS_PAD)
    own = order(tab, all_pts, span)
    other = lax.ppermute(own, "c", swap)
    cross, p_cross, psq, p_oth = first_half(info, points, own)
    wh, wl = inverse(info, tab, p_oth, other, cross, p_cross, psq, share)
    all_res, wh = lax.optimization_barrier((all_res, wh))
    other_res = lax.ppermute(all_res, "c", swap)
    hi, lo, change = update_own(tab, wh, wl, all_res, span)
    out_t, step_share = update_other(info, hi, lo, other_res, change, res_t, share)
    return (out_t.T, step_share)


def solution(mesh):
    fine = Mesh(mesh.devices.reshape(4, 4, 2, 8, 2), EVERY)
    return jax.shard_map(
        on_device,
        mesh=fine,
        in_specs=(P(EVERY, None), P(EVERY, None), P()),
        out_specs=(P(EVERY, None), P(("zl", "c"), None)),
        check_vma=False,
    )
```

```python
import functools

import jax
import jax.numpy as jnp
from jax import lax
from jax.experimental import pallas as pl
from jax.experimental.pallas import tpu as pltpu
from jax.sharding import Mesh
from jax.sharding import PartitionSpec as P

F32 = jnp.float32
BF = jnp.bfloat16
I32 = jnp.int32
HI = lax.Precision.HIGHEST
NN = (((1,), (0,)), ((), ()))
NT = (((1,), (1,)), ((), ()))
TN = (((0,), (0,)), ((), ()))

GAMMA = 0.125
RIDGE = 0.5
PLANE = ("y", "x")
COLUMN = ("zh", "zl", "c")
EVERY = PLANE + COLUMN
CAP = 2
COL_CAP = 48
CLASS_PAD = 1024
SPLIT = 4
MIB = 1024 * 1024


def dot(a, b, dn=NN, prec=None):
    return lax.dot_general(a, b, dn, preferred_element_type=F32, precision=prec)


def iota(shape, axis):
    return lax.broadcasted_iota(I32, shape, axis)


def two_parts(v):
    hi = v.astype(BF)
    return hi, (v - hi.astype(F32)).astype(BF)


def mm3(a, b):
    ah, al = a
    bh, bl = b
    return dot(ah, bh) + (dot(ah, bl) + dot(al, bh))


def vmem():
    return pl.BlockSpec(memory_space=pltpu.VMEM)


def smem():
    return pl.BlockSpec(memory_space=pltpu.SMEM)


def hbm():
    return pl.BlockSpec(memory_space=pltpu.HBM)


def params(mib):
    return pltpu.CompilerParams(vmem_limit_bytes=mib * MIB)


def pack_body(info, ids_hbm, pts_hbm, res_hbm, out_ref, tab_ref, ids_ref, pts_ref, res_ref, sems, *, n_plane, n_col):
    me = info[2]
    rows = pts_ref.shape[0]
    ids_in = pltpu.make_async_copy(ids_hbm, ids_ref, sems.at[0])
    pts_in = pltpu.make_async_copy(pts_hbm, pts_ref, sems.at[1])
    res_in = pltpu.make_async_copy(res_hbm, res_ref, sems.at[2])
    ids_in.start()
    pts_in.start()
    res_in.start()
    ids_in.wait()
    ids = ids_ref[...]
    n = ids.shape[1]
    eye = iota((n, n), 0) == iota((n, n), 1)
    ids_col = jnp.sum(jnp.where(eye, jnp.broadcast_to(ids, (n, n)), 0), axis=1, keepdims=True)
    owner = ids // rows
    column = ids // (rows * n_col)
    less = jnp.broadcast_to(ids_col, (n, n)) < ids
    rank = jnp.sum(jnp.where(less & (ids_col >= column * (rows * n_col)), 1, 0), axis=0, keepdims=True)
    slot = jnp.sum(jnp.where(less & (ids_col >= owner * rows), 1, 0), axis=0, keepdims=True)
    planes = COL_CAP * n_plane
    straight = column * COL_CAP + rank
    turned = planes - COL_CAP - column * COL_CAP + rank
    here = jnp.where(info[0] == 0, straight, turned)
    there = jnp.where(info[0] == 0, turned, straight)
    tab_ref[...] = jnp.concatenate([ids, rank, slot, here, there, jnp.zeros((3, n), I32)], axis=0)
    mine = owner == me
    lane = iota((8, rows), 1)
    sub = iota((8, rows), 0)
    take = jnp.zeros((8, rows), F32)
    for k in range(CAP):
        at = jnp.max(jnp.where(mine & (slot == k), ids - me * rows, -1), axis=1, keepdims=True)
        take = jnp.where((sub == k) & (lane == at), 1.0, take)
    take = take.astype(BF)
    pts_in.wait()
    picked = dot(take, pts_ref[...]).astype(BF)
    res_in.wait()
    res = res_ref[...]
    hi = res.astype(BF)
    low = (res - hi.astype(F32)).astype(BF)
    classes = res.shape[0]
    pad = jnp.zeros((8, CLASS_PAD - classes), F32)
    parts = [jnp.concatenate([dot(take, v, NT), pad], axis=1).astype(BF) for v in (hi, low)]
    half = pts_ref.shape[1] // 2
    chalf = CLASS_PAD // 2
    for core in range(2):
        row = [picked[:CAP, core * half : (core + 1) * half]]
        row += [v[:CAP, core * chalf : (core + 1) * chalf] for v in parts]
        row = jnp.concatenate(row, axis=1).astype(F32)
        w = row.shape[1] // SPLIT
        block = jnp.concatenate([row[:, q * w : (q + 1) * w] for q in range(SPLIT)], axis=0).astype(BF)
        for z in range(n_col // 2):
            out_ref[2 * z + core] = block


def pack(info, ids, points, res_t, n_plane, n_col):
    width = points.shape[1] // 2 + CLASS_PAD
    n = ids.shape[1]
    return pl.pallas_call(
        functools.partial(pack_body, n_plane=n_plane, n_col=n_col),
        out_shape=(
            jax.ShapeDtypeStruct((n_col, CAP * SPLIT, width // SPLIT), BF),
            jax.ShapeDtypeStruct((8, n), I32),
        ),
        in_specs=[smem(), hbm(), hbm(), hbm()],
        out_specs=(vmem(), vmem()),
        scratch_shapes=[
            pltpu.VMEM(ids.shape, I32),
            pltpu.VMEM(points.shape, BF),
            pltpu.VMEM(res_t.shape, F32),
            pltpu.SemaphoreType.DMA((3,)),
        ],
        compiler_params=params(60),
    )(info, ids, points, res_t)


def table(tab_ref):
    return tab_ref[0:1, :], tab_ref[1:2, :], tab_ref[2:3, :]


def compact_body(info, tab_ref, in_ref, pts_ref, res_ref, *, rows, n_col):
    plane = info[1]
    ids, rank, slot = table(tab_ref)
    n = ids.shape[1]
    owner = ids // rows
    column = ids // (rows * n_col)
    wide = in_ref.shape[0]
    sel_rank = (iota((COL_CAP, n), 0) == rank) & (column == plane)
    at = iota((wide, n), 0)
    group = CAP * SPLIT
    sel_slot = (at // group == owner - column * n_col) & (at % CAP == slot)
    pick = dot(sel_rank.astype(F32).astype(BF), sel_slot.astype(F32).astype(BF), NT)
    part = (iota((COL_CAP, wide), 1) // CAP) % SPLIT
    data = in_ref[...]
    whole = [dot(jnp.where(part == q, pick, 0.0).astype(BF), data) for q in range(SPLIT)]
    whole = jnp.concatenate(whole, axis=1)
    half = pts_ref.shape[2]
    pts = whole[:, :half].astype(BF)
    res = whole[:, half:].astype(BF)
    for p in range(pts_ref.shape[0]):
        pts_ref[p] = pts
        res_ref[p] = res


def compact(info, tab, data, rows, half, n_plane, n_col):
    return pl.pallas_call(
        functools.partial(compact_body, rows=rows, n_col=n_col),
        out_shape=(
            jax.ShapeDtypeStruct((n_plane, COL_CAP, half), BF),
            jax.ShapeDtypeStruct((n_plane, COL_CAP, CLASS_PAD), BF),
        ),
        in_specs=[smem(), vmem(), vmem()],
        out_specs=(vmem(), vmem()),
        compiler_params=params(16),
    )(info, tab, data)


def place_matrix(tab_ref, wide, row=3):
    at = tab_ref[row : row + 1, :]
    return (iota((wide, at.shape[1]), 0) == at).astype(F32).astype(BF)


def order_body(tab_ref, in_ref, out_ref):
    out_ref[...] = dot(place_matrix(tab_ref, in_ref.shape[0]), in_ref[...], TN).astype(BF)


def order(tab, data):
    return pl.pallas_call(
        order_body,
        out_shape=jax.ShapeDtypeStruct((tab.shape[1], data.shape[1]), BF),
        in_specs=[vmem(), vmem()],
        out_specs=vmem(),
        compiler_params=params(10),
    )(tab, data)


def first_half_body(info, pts_ref, own_ref, cross_ref, p_cross_ref, psq_ref, p_oth_ref, *, half):
    core = info[0]
    own = own_ref[...]
    cross_ref[...] = dot(own, own, NT)
    p_own = pts_ref[:, pl.ds(pl.multiple_of(core * half, half), half)]
    p_oth = pts_ref[:, pl.ds(pl.multiple_of((1 - core) * half, half), half)]
    p_cross_ref[...] = dot(p_own, own, NT)
    p_oth_ref[...] = p_oth
    a = p_own.astype(F32)
    b = p_oth.astype(F32)
    psq_ref[...] = jnp.sum(a * a, axis=1, keepdims=True) + jnp.sum(b * b, axis=1, keepdims=True)


def first_half(info, points, own):
    n, half = own.shape
    rows = points.shape[0]
    return pl.pallas_call(
        functools.partial(first_half_body, half=half),
        out_shape=(
            jax.ShapeDtypeStruct((n, n), F32),
            jax.ShapeDtypeStruct((rows, n), F32),
            jax.ShapeDtypeStruct((rows, 1), F32),
            jax.ShapeDtypeStruct((rows, half), BF),
        ),
        in_specs=[smem(), vmem(), vmem()],
        out_specs=(vmem(),) * 4,
        compiler_params=params(12),
        cost_estimate=pl.CostEstimate(flops=10**6, bytes_accessed=10**6, transcendentals=0),
    )(info, points, own)


def inverse_body(info, tab_ref, p_oth_ref, oth_ref, cross_ref, p_cross_ref, psq_ref, hi_ref, lo_ref, g_ref, m_ref, gh_ref, gl_ref, x_ref, *, share):
    n = oth_ref.shape[0]
    rows = p_cross_ref.shape[0]
    me, share_at = info[2], info[3]
    oth = oth_ref[...]
    cross = cross_ref[...] + dot(oth, oth, NT)
    eye = iota((n, n), 0) == iota((n, n), 1)
    diag = jnp.where(eye, cross, 0.0)
    sq_row = jnp.sum(diag, axis=0, keepdims=True)
    sq_col = jnp.sum(diag, axis=1, keepdims=True)
    gram = jnp.exp(-GAMMA * (sq_col + sq_row - 2.0 * cross)) + jnp.where(eye, RIDGE, 0.0)
    g_ref[...] = gram
    gh, gl = two_parts(gram)
    gh_ref[...] = gh
    gl_ref[...] = gl
    p_cross = p_cross_ref[...] + dot(p_oth_ref[...], oth, NT)
    p_kern = jnp.exp(-GAMMA * (psq_ref[...] + sq_row - 2.0 * p_cross))
    point_id = me * rows + iota((rows, n), 0)
    m_ref[pl.ds(0, rows), :] = p_kern + jnp.where(point_id == table(tab_ref)[0], RIDGE, 0.0)
    m_ref[pl.ds(rows, share), :] = jnp.where(share_at + iota((share, n), 0) == iota((share, n), 1), 1.0, 0.0)
    lo = 0.499
    gram = g_ref[...]
    v_col = jnp.sum(gram, axis=1, keepdims=True)
    v_row = jnp.sum(gram, axis=0, keepdims=True)
    hi = jnp.max(jnp.sum(gram * v_col, axis=0, keepdims=True) / v_row) * 1.001
    s = 2.0 / (lo + hi)
    x_ref[...] = jnp.where(eye, 2.0 * s, 0.0) - (s * s) * gram
    d = (hi - lo) / (hi + lo)

    def refine(resid):
        x = x_ref[...] * (2.0 / (2.0 - resid))
        xh, xl = two_parts(x)
        r = (jnp.where(eye, 1.0, 0.0) - mm3((gh_ref[...], gl_ref[...]), (xh, xl))).astype(BF)
        x_ref[...] = x + (dot(xh, r) + dot(xl, r))
        after = resid / (2.0 - resid)
        return after * after

    lax.while_loop(lambda resid: resid > 5e-4, refine, d * d)
    xs = two_parts(x_ref[...])
    m = m_ref[...]
    w = mm3(two_parts(m), xs)
    e = m - dot(w, g_ref[...], NN, HI)
    w = w + mm3(two_parts(e), xs)
    wh, wl = two_parts(w)
    hi_ref[...] = wh
    lo_ref[...] = wl


def inverse(info, tab, p_oth, oth, cross, p_cross, psq, share):
    n = oth.shape[0]
    rows = p_oth.shape[0]
    out = jax.ShapeDtypeStruct((rows + share, n), BF)
    return pl.pallas_call(
        functools.partial(inverse_body, share=share),
        out_shape=(out, out),
        in_specs=[smem()] + [vmem()] * 6,
        out_specs=(vmem(), vmem()),
        scratch_shapes=[
            pltpu.VMEM((n, n), F32),
            pltpu.VMEM((rows + share, n), F32),
            pltpu.VMEM((n, n), BF),
            pltpu.VMEM((n, n), BF),
            pltpu.VMEM((n, n), F32),
        ],
        compiler_params=params(18),
        cost_estimate=pl.CostEstimate(flops=10**6, bytes_accessed=10**6, transcendentals=0),
    )(info, tab, p_oth, oth, cross, p_cross, psq)


def apply_weights(hi, lo, res_ref):
    chalf = res_ref.shape[1] // 2
    return mm3((hi, lo), (res_ref[:, :chalf], res_ref[:, chalf:]))


def update_own_body(tab_ref, wh_ref, wl_ref, res_ref, hi_ref, lo_ref, ch_ref):
    wide = res_ref.shape[0]
    here = place_matrix(tab_ref, wide)
    hi = dot(wh_ref[...], here, NT).astype(BF)
    lo = dot(wl_ref[...], here, NT).astype(BF)
    ch_ref[...] = apply_weights(hi, lo, res_ref)
    there = place_matrix(tab_ref, wide, 4)
    hi_ref[...] = dot(wh_ref[...], there, NT).astype(BF)
    lo_ref[...] = dot(wl_ref[...], there, NT).astype(BF)


def update_own(tab, wh, wl, res):
    m = wh.shape[0]
    wide, parts = res.shape
    out = jax.ShapeDtypeStruct((m, wide), BF)
    return pl.pallas_call(
        update_own_body,
        out_shape=(out, out, jax.ShapeDtypeStruct((m, parts // 2), F32)),
        in_specs=[vmem()] * 4,
        out_specs=(vmem(),) * 3,
        compiler_params=params(10),
        cost_estimate=pl.CostEstimate(flops=2 * 10**9, bytes_accessed=4 * 10**6, transcendentals=0),
    )(tab, wh, wl, res)


def update_other_body(info, hi_ref, lo_ref, res_ref, ch_ref, res_t_ref, out_ref, share_ref, all_ref):
    core = info[0]
    classes, rows = res_t_ref.shape
    chalf = ch_ref.shape[1]
    all_ref[:, pl.ds(pl.multiple_of(core * chalf, chalf), chalf)] = ch_ref[...]
    change = apply_weights(hi_ref[...], lo_ref[...], res_ref)
    all_ref[:, pl.ds(pl.multiple_of((1 - core) * chalf, chalf), chalf)] = change
    share_ref[...] = all_ref[pl.ds(rows, share_ref.shape[0]), pl.ds(0, classes)]
    out_ref[...] = res_t_ref[...] - all_ref[pl.ds(0, rows), :].T[:classes]


def update_other(info, hi, lo, res, change, res_t, share):
    classes, rows = res_t.shape
    return pl.pallas_call(
        update_other_body,
        out_shape=(jax.ShapeDtypeStruct((classes, rows), F32), jax.ShapeDtypeStruct((share, classes), F32)),
        in_specs=[smem()] + [vmem()] * 5,
        out_specs=(vmem(), vmem()),
        scratch_shapes=[pltpu.VMEM((rows + share, CLASS_PAD), F32)],
        compiler_params=params(16),
    )(info, hi, lo, res, change, res_t)


def plane_groups():
    groups = []
    for place in range(32):
        members = [p * 32 + place for p in range(16)]
        groups.append(members if place % 2 == 0 else members[::-1])
    return groups


def over_plane(value):
    return lax.all_to_all(value, EVERY, 0, 0, axis_index_groups=plane_groups(), tiled=True)


def on_device(points, residual, block_ids):
    rows, feats = points.shape
    block = block_ids.shape[0]
    n_plane = lax.axis_size(PLANE)
    n_col = lax.axis_size(COLUMN)
    n_gy = lax.axis_size("zl") * lax.axis_size("c")
    plane = lax.axis_index(PLANE)
    place = lax.axis_index(COLUMN)
    share = block // n_gy
    half = feats // 2
    wide = n_plane * COL_CAP
    info = jnp.stack([lax.axis_index("c"), plane, plane * n_col + place, (place % n_gy) * share]).astype(I32)
    ids = block_ids.reshape(1, block)
    res_t = residual.T
    swap = [(0, 1), (1, 0)]

    packed, tab = pack(info, ids, points, res_t, n_plane, n_col)
    col_rows = lax.all_to_all(packed, COLUMN, 0, 0, tiled=True)
    col_rows = col_rows.reshape(n_col * CAP * SPLIT, col_rows.shape[2])
    pts_out, res_out = compact(info, tab, col_rows, rows, half, n_plane, n_col)
    all_pts = over_plane(pts_out).reshape(wide, half)
    all_res = over_plane(res_out).reshape(wide, CLASS_PAD)
    own = order(tab, all_pts)
    other = lax.ppermute(own, "c", swap)
    cross, p_cross, psq, p_oth = first_half(info, points, own)
    wh, wl = inverse(info, tab, p_oth, other, cross, p_cross, psq, share)
    all_res, wh = lax.optimization_barrier((all_res, wh))
    other_res = lax.ppermute(all_res, "c", swap)
    hi, lo, change = update_own(tab, wh, wl, all_res)
    out_t, step_share = update_other(info, hi, lo, other_res, change, res_t, share)
    return (out_t.T, step_share)


def solution(mesh):
    fine = Mesh(mesh.devices.reshape(4, 4, 2, 8, 2), EVERY)
    return jax.shard_map(
        on_device,
        mesh=fine,
        in_specs=(P(EVERY, None), P(EVERY, None), P()),
        out_specs=(P(EVERY, None), P(("zl", "c"), None)),
        check_vma=False,
    )
```

```python
import functools

import jax
import jax.numpy as jnp
from jax import lax
from jax.experimental import pallas as pl
from jax.experimental.pallas import tpu as pltpu
from jax.sharding import Mesh
from jax.sharding import PartitionSpec as P

F32 = jnp.float32
BF = jnp.bfloat16
I32 = jnp.int32
HI = lax.Precision.HIGHEST
NN = (((1,), (0,)), ((), ()))
NT = (((1,), (1,)), ((), ()))
TN = (((0,), (0,)), ((), ()))

GAMMA = 0.125
RIDGE = 0.5
PLANE = ("y", "x")
COLUMN = ("zh", "zl", "c")
EVERY = PLANE + COLUMN
CAP = 2
COL_CAP = 48
CLASS_PAD = 1024
SPLIT = 4
CLASS_STEP = 496
CLASS_SPAN = 504
MIB = 1024 * 1024


def dot(a, b, dn=NN, prec=None):
    return lax.dot_general(a, b, dn, preferred_element_type=F32, precision=prec)


def iota(shape, axis):
    return lax.broadcasted_iota(I32, shape, axis)


def two_parts(v):
    hi = v.astype(BF)
    return hi, (v - hi.astype(F32)).astype(BF)


def mm3(a, b):
    ah, al = a
    bh, bl = b
    return dot(ah, bh) + (dot(ah, bl) + dot(al, bh))


def vmem():
    return pl.BlockSpec(memory_space=pltpu.VMEM)


def smem():
    return pl.BlockSpec(memory_space=pltpu.SMEM)


def hbm():
    return pl.BlockSpec(memory_space=pltpu.HBM)


def params(mib):
    return pltpu.CompilerParams(vmem_limit_bytes=mib * MIB)


def pack_body(info, ids_hbm, pts_hbm, res_hbm, out_ref, tab_ref, ids_ref, pts_ref, res_ref, sems, *, n_plane, n_col):
    me = info[2]
    rows = pts_ref.shape[0]
    ids_in = pltpu.make_async_copy(ids_hbm, ids_ref, sems.at[0])
    pts_in = pltpu.make_async_copy(pts_hbm, pts_ref, sems.at[1])
    res_in = pltpu.make_async_copy(res_hbm, res_ref, sems.at[2])
    ids_in.start()
    pts_in.start()
    res_in.start()
    ids_in.wait()
    ids = ids_ref[...]
    n = ids.shape[1]
    eye = iota((n, n), 0) == iota((n, n), 1)
    ids_col = jnp.sum(jnp.where(eye, jnp.broadcast_to(ids, (n, n)), 0), axis=1, keepdims=True)
    owner = ids // rows
    column = ids // (rows * n_col)
    less = jnp.broadcast_to(ids_col, (n, n)) < ids
    rank = jnp.sum(jnp.where(less & (ids_col >= column * (rows * n_col)), 1, 0), axis=0, keepdims=True)
    slot = jnp.sum(jnp.where(less & (ids_col >= owner * rows), 1, 0), axis=0, keepdims=True)
    planes = COL_CAP * n_plane
    straight = column * COL_CAP + rank
    turned = planes - COL_CAP - column * COL_CAP + rank
    here = jnp.where(info[0] == 0, straight, turned)
    there = jnp.where(info[0] == 0, turned, straight)
    tab_ref[...] = jnp.concatenate([ids, rank, slot, here, there, jnp.zeros((3, n), I32)], axis=0)
    mine = owner == me
    lane = iota((8, rows), 1)
    sub = iota((8, rows), 0)
    take = jnp.zeros((8, rows), F32)
    for k in range(CAP):
        at = jnp.max(jnp.where(mine & (slot == k), ids - me * rows, -1), axis=1, keepdims=True)
        take = jnp.where((sub == k) & (lane == at), 1.0, take)
    take = take.astype(BF)
    pts_in.wait()
    picked = dot(take, pts_ref[...]).astype(BF)
    res_in.wait()
    res = res_ref[...]
    hi = res.astype(BF)
    low = (res - hi.astype(F32)).astype(BF)
    classes = res.shape[0]
    pad = jnp.zeros((8, CLASS_PAD - classes), F32)
    parts = [jnp.concatenate([dot(take, v, NT), pad], axis=1).astype(BF) for v in (hi, low)]
    half = pts_ref.shape[1] // 2
    chalf = CLASS_PAD // 2
    for core in range(2):
        row = [picked[:CAP, core * half : (core + 1) * half]]
        row += [v[:CAP, core * CLASS_STEP : core * CLASS_STEP + chalf] for v in parts]
        row = jnp.concatenate(row, axis=1).astype(F32)
        w = row.shape[1] // SPLIT
        block = jnp.concatenate([row[:, q * w : (q + 1) * w] for q in range(SPLIT)], axis=0).astype(BF)
        for z in range(n_col // 2):
            out_ref[2 * z + core] = block


def pack(info, ids, points, res_t, n_plane, n_col):
    width = points.shape[1] // 2 + CLASS_PAD
    n = ids.shape[1]
    return pl.pallas_call(
        functools.partial(pack_body, n_plane=n_plane, n_col=n_col),
        out_shape=(
            jax.ShapeDtypeStruct((n_col, CAP * SPLIT, width // SPLIT), BF),
            jax.ShapeDtypeStruct((8, n), I32),
        ),
        in_specs=[smem(), hbm(), hbm(), hbm()],
        out_specs=(vmem(), vmem()),
        scratch_shapes=[
            pltpu.VMEM(ids.shape, I32),
            pltpu.VMEM(points.shape, BF),
            pltpu.VMEM(res_t.shape, F32),
            pltpu.SemaphoreType.DMA((3,)),
        ],
        compiler_params=params(60),
    )(info, ids, points, res_t)


def table(tab_ref):
    return tab_ref[0:1, :], tab_ref[1:2, :], tab_ref[2:3, :]


def compact_body(info, tab_ref, in_ref, pts_ref, res_ref, *, rows, n_col):
    plane = info[1]
    ids, rank, slot = table(tab_ref)
    n = ids.shape[1]
    owner = ids // rows
    column = ids // (rows * n_col)
    wide = in_ref.shape[0]
    sel_rank = (iota((COL_CAP, n), 0) == rank) & (column == plane)
    at = iota((wide, n), 0)
    group = CAP * SPLIT
    sel_slot = (at // group == owner - column * n_col) & (at % CAP == slot)
    pick = dot(sel_rank.astype(F32).astype(BF), sel_slot.astype(F32).astype(BF), NT)
    part = (iota((COL_CAP, wide), 1) // CAP) % SPLIT
    data = in_ref[...]
    whole = [dot(jnp.where(part == q, pick, 0.0).astype(BF), data) for q in range(SPLIT)]
    whole = jnp.concatenate(whole, axis=1)
    half = pts_ref.shape[2]
    pts = whole[:, :half].astype(BF)
    res = whole[:, half:].astype(BF)
    for p in range(pts_ref.shape[0]):
        pts_ref[p] = pts
        res_ref[p] = res


def compact(info, tab, data, rows, half, n_plane, n_col):
    return pl.pallas_call(
        functools.partial(compact_body, rows=rows, n_col=n_col),
        out_shape=(
            jax.ShapeDtypeStruct((n_plane, COL_CAP, half), BF),
            jax.ShapeDtypeStruct((n_plane, COL_CAP, CLASS_PAD), BF),
        ),
        in_specs=[smem(), vmem(), vmem()],
        out_specs=(vmem(), vmem()),
        compiler_params=params(16),
    )(info, tab, data)


def place_matrix(tab_ref, wide, row=3):
    at = tab_ref[row : row + 1, :]
    return (iota((wide, at.shape[1]), 0) == at).astype(F32).astype(BF)


def order_body(tab_ref, in_ref, out_ref):
    out_ref[...] = dot(place_matrix(tab_ref, in_ref.shape[0]), in_ref[...], TN).astype(BF)


def order(tab, data):
    return pl.pallas_call(
        order_body,
        out_shape=jax.ShapeDtypeStruct((tab.shape[1], data.shape[1]), BF),
        in_specs=[vmem(), vmem()],
        out_specs=vmem(),
        compiler_params=params(10),
    )(tab, data)


def first_half_body(info, pts_ref, own_ref, cross_ref, p_cross_ref, psq_ref, p_oth_ref, *, half):
    core = info[0]
    own = own_ref[...]
    cross_ref[...] = dot(own, own, NT)
    p_own = pts_ref[:, pl.ds(pl.multiple_of(core * half, half), half)]
    p_oth = pts_ref[:, pl.ds(pl.multiple_of((1 - core) * half, half), half)]
    p_cross_ref[...] = dot(p_own, own, NT)
    p_oth_ref[...] = p_oth
    a = p_own.astype(F32)
    b = p_oth.astype(F32)
    psq_ref[...] = jnp.sum(a * a, axis=1, keepdims=True) + jnp.sum(b * b, axis=1, keepdims=True)


def first_half(info, points, own):
    n, half = own.shape
    rows = points.shape[0]
    return pl.pallas_call(
        functools.partial(first_half_body, half=half),
        out_shape=(
            jax.ShapeDtypeStruct((n, n), F32),
            jax.ShapeDtypeStruct((rows, n), F32),
            jax.ShapeDtypeStruct((rows, 1), F32),
            jax.ShapeDtypeStruct((rows, half), BF),
        ),
        in_specs=[smem(), vmem(), vmem()],
        out_specs=(vmem(),) * 4,
        compiler_params=params(12),
        cost_estimate=pl.CostEstimate(flops=10**6, bytes_accessed=10**6, transcendentals=0),
    )(info, points, own)


def inverse_body(info, tab_ref, p_oth_ref, oth_ref, cross_ref, p_cross_ref, psq_ref, hi_ref, lo_ref, g_ref, m_ref, gh_ref, gl_ref, x_ref, *, share):
    n = oth_ref.shape[0]
    rows = p_cross_ref.shape[0]
    me, share_at = info[2], info[3]
    oth = oth_ref[...]
    cross = cross_ref[...] + dot(oth, oth, NT)
    eye = iota((n, n), 0) == iota((n, n), 1)
    diag = jnp.where(eye, cross, 0.0)
    sq_row = jnp.sum(diag, axis=0, keepdims=True)
    sq_col = jnp.sum(diag, axis=1, keepdims=True)
    gram = jnp.exp(-GAMMA * (sq_col + sq_row - 2.0 * cross)) + jnp.where(eye, RIDGE, 0.0)
    g_ref[...] = gram
    gh, gl = two_parts(gram)
    gh_ref[...] = gh
    gl_ref[...] = gl
    p_cross = p_cross_ref[...] + dot(p_oth_ref[...], oth, NT)
    p_kern = jnp.exp(-GAMMA * (psq_ref[...] + sq_row - 2.0 * p_cross))
    point_id = me * rows + iota((rows, n), 0)
    m_ref[pl.ds(0, rows), :] = p_kern + jnp.where(point_id == table(tab_ref)[0], RIDGE, 0.0)
    m_ref[pl.ds(rows, share), :] = jnp.where(share_at + iota((share, n), 0) == iota((share, n), 1), 1.0, 0.0)
    lo = 0.499
    gram = g_ref[...]
    v_col = jnp.sum(gram, axis=1, keepdims=True)
    v_row = jnp.sum(gram, axis=0, keepdims=True)
    hi = jnp.max(jnp.sum(gram * v_col, axis=0, keepdims=True) / v_row) * 1.001
    s = 2.0 / (lo + hi)
    x_ref[...] = jnp.where(eye, 2.0 * s, 0.0) - (s * s) * gram
    d = (hi - lo) / (hi + lo)

    def refine(resid):
        x = x_ref[...] * (2.0 / (2.0 - resid))
        xh, xl = two_parts(x)
        r = (jnp.where(eye, 1.0, 0.0) - mm3((gh_ref[...], gl_ref[...]), (xh, xl))).astype(BF)
        x_ref[...] = x + (dot(xh, r) + dot(xl, r))
        after = resid / (2.0 - resid)
        return after * after

    lax.while_loop(lambda resid: resid > 5e-4, refine, d * d)
    xs = two_parts(x_ref[...])
    m = m_ref[...]
    w = mm3(two_parts(m), xs)
    e = m - dot(w, g_ref[...], NN, HI)
    w = w + mm3(two_parts(e), xs)
    wh, wl = two_parts(w)
    hi_ref[...] = wh
    lo_ref[...] = wl


def inverse(info, tab, p_oth, oth, cross, p_cross, psq, share):
    n = oth.shape[0]
    rows = p_oth.shape[0]
    out = jax.ShapeDtypeStruct((rows + share, n), BF)
    return pl.pallas_call(
        functools.partial(inverse_body, share=share),
        out_shape=(out, out),
        in_specs=[smem()] + [vmem()] * 6,
        out_specs=(vmem(), vmem()),
        scratch_shapes=[
            pltpu.VMEM((n, n), F32),
            pltpu.VMEM((rows + share, n), F32),
            pltpu.VMEM((n, n), BF),
            pltpu.VMEM((n, n), BF),
            pltpu.VMEM((n, n), F32),
        ],
        compiler_params=params(18),
        cost_estimate=pl.CostEstimate(flops=10**6, bytes_accessed=10**6, transcendentals=0),
    )(info, tab, p_oth, oth, cross, p_cross, psq)


def apply_weights(hi, lo, res_ref):
    chalf = res_ref.shape[1] // 2
    return mm3((hi, lo), (res_ref[:, :chalf], res_ref[:, chalf:]))


def write_half(which, change, res_t_ref, out_hbm, buf, sem):
    rows = res_t_ref.shape[1]
    span = pl.ds(pl.multiple_of(which * CLASS_STEP, 8), CLASS_SPAN)
    buf[...] = res_t_ref[span, :] - change[:rows].T[:CLASS_SPAN]
    copy = pltpu.make_async_copy(buf, out_hbm.at[span, :], sem)
    copy.start()
    return copy


def update_own_body(info, tab_ref, wh_ref, wl_ref, res_ref, res_t_ref, hi_ref, lo_ref, part_ref, out_hbm, buf, sem):
    rows = res_t_ref.shape[1]
    wide = res_ref.shape[0]
    here = place_matrix(tab_ref, wide)
    hi = dot(wh_ref[...], here, NT).astype(BF)
    lo = dot(wl_ref[...], here, NT).astype(BF)
    change = apply_weights(hi, lo, res_ref)
    part_ref[...] = change[rows:]
    copy = write_half(info[0], change, res_t_ref, out_hbm, buf, sem)
    there = place_matrix(tab_ref, wide, 4)
    hi_ref[...] = dot(wh_ref[...], there, NT).astype(BF)
    lo_ref[...] = dot(wl_ref[...], there, NT).astype(BF)
    copy.wait()


def half_scratch(rows):
    return [pltpu.VMEM((CLASS_SPAN, rows), F32), pltpu.SemaphoreType.DMA(())]


def update_own(info, tab, wh, wl, res, res_t):
    m = wh.shape[0]
    wide, parts = res.shape
    classes, rows = res_t.shape
    out = jax.ShapeDtypeStruct((m, wide), BF)
    return pl.pallas_call(
        update_own_body,
        out_shape=(
            out,
            out,
            jax.ShapeDtypeStruct((m - rows, parts // 2), F32),
            jax.ShapeDtypeStruct((classes, rows), F32),
        ),
        in_specs=[smem()] + [vmem()] * 5,
        out_specs=(vmem(), vmem(), vmem(), hbm()),
        scratch_shapes=half_scratch(rows),
        compiler_params=params(12),
        cost_estimate=pl.CostEstimate(flops=2 * 10**9, bytes_accessed=4 * 10**6, transcendentals=0),
    )(info, tab, wh, wl, res, res_t)


def update_other_body(info, hi_ref, lo_ref, res_ref, part_ref, res_t_ref, begun_hbm, out_hbm, share_ref, buf, sem):
    core = info[0]
    classes, rows = res_t_ref.shape
    change = apply_weights(hi_ref[...], lo_ref[...], res_ref)
    copy = write_half(1 - core, change, res_t_ref, out_hbm, buf, sem)
    mine, theirs = part_ref[...], change[rows:]
    low = jnp.where(core == 0, mine, theirs)
    high = jnp.where(core == 0, theirs, mine)
    share_ref[...] = jnp.concatenate([low[:, :CLASS_SPAN], high[:, 2 * CLASS_SPAN - classes : CLASS_SPAN]], axis=1)
    copy.wait()


def update_other(info, hi, lo, res, part, res_t, begun):
    classes, rows = res_t.shape
    return pl.pallas_call(
        update_other_body,
        out_shape=(jax.ShapeDtypeStruct((classes, rows), F32), jax.ShapeDtypeStruct((part.shape[0], classes), F32)),
        in_specs=[smem()] + [vmem()] * 5 + [hbm()],
        out_specs=(hbm(), vmem()),
        input_output_aliases={6: 0},
        scratch_shapes=half_scratch(rows),
        compiler_params=params(12),
    )(info, hi, lo, res, part, res_t, begun)


def plane_groups():
    groups = []
    for place in range(32):
        members = [p * 32 + place for p in range(16)]
        groups.append(members if place % 2 == 0 else members[::-1])
    return groups


def over_plane(value):
    return lax.all_to_all(value, EVERY, 0, 0, axis_index_groups=plane_groups(), tiled=True)


def on_device(points, residual, block_ids):
    rows, feats = points.shape
    block = block_ids.shape[0]
    n_plane = lax.axis_size(PLANE)
    n_col = lax.axis_size(COLUMN)
    n_gy = lax.axis_size("zl") * lax.axis_size("c")
    plane = lax.axis_index(PLANE)
    place = lax.axis_index(COLUMN)
    share = block // n_gy
    half = feats // 2
    wide = n_plane * COL_CAP
    info = jnp.stack([lax.axis_index("c"), plane, plane * n_col + place, (place % n_gy) * share]).astype(I32)
    ids = block_ids.reshape(1, block)
    res_t = residual.T
    swap = [(0, 1), (1, 0)]

    packed, tab = pack(info, ids, points, res_t, n_plane, n_col)
    col_rows = lax.all_to_all(packed, COLUMN, 0, 0, tiled=True)
    col_rows = col_rows.reshape(n_col * CAP * SPLIT, col_rows.shape[2])
    pts_out, res_out = compact(info, tab, col_rows, rows, half, n_plane, n_col)
    all_pts = over_plane(pts_out).reshape(wide, half)
    all_res = over_plane(res_out).reshape(wide, CLASS_PAD)
    own = order(tab, all_pts)
    other = lax.ppermute(own, "c", swap)
    cross, p_cross, psq, p_oth = first_half(info, points, own)
    wh, wl = inverse(info, tab, p_oth, other, cross, p_cross, psq, share)
    all_res, wh = lax.optimization_barrier((all_res, wh))
    other_res = lax.ppermute(all_res, "c", swap)
    hi, lo, part, begun = update_own(info, tab, wh, wl, all_res, res_t)
    out_t, step_share = update_other(info, hi, lo, other_res, part, res_t, begun)
    return (out_t.T, step_share)


def solution(mesh):
    fine = Mesh(mesh.devices.reshape(4, 4, 2, 8, 2), EVERY)
    return jax.shard_map(
        on_device,
        mesh=fine,
        in_specs=(P(EVERY, None), P(EVERY, None), P()),
        out_specs=(P(EVERY, None), P(("zl", "c"), None)),
        check_vma=False,
    )
```

```python
import functools

import jax
import jax.numpy as jnp
from jax import lax
from jax.experimental import pallas as pl
from jax.experimental.pallas import tpu as pltpu
from jax.sharding import Mesh
from jax.sharding import PartitionSpec as P

F32 = jnp.float32
BF = jnp.bfloat16
I32 = jnp.int32
HI = lax.Precision.HIGHEST
NN = (((1,), (0,)), ((), ()))
NT = (((1,), (1,)), ((), ()))
TN = (((0,), (0,)), ((), ()))

GAMMA = 0.125
RIDGE = 0.5
PLANE = ("y", "x")
COLUMN = ("zh", "zl", "c")
EVERY = PLANE + COLUMN
CAP = 2
COL_CAP = 48
CLASS_PAD = 1024
SPLIT = 4
CLASS_STEP = 496
CLASS_SPAN = 504
SCALE_LANE = 511
FRACTION = 2.0**22
MIB = 1024 * 1024


def dot(a, b, dn=NN, prec=None):
    return lax.dot_general(a, b, dn, preferred_element_type=F32, precision=prec)


def iota(shape, axis):
    return lax.broadcasted_iota(I32, shape, axis)


def two_parts(v):
    hi = v.astype(BF)
    return hi, (v - hi.astype(F32)).astype(BF)


def mm3(a, b):
    ah, al = a
    bh, bl = b
    return dot(ah, bh) + (dot(ah, bl) + dot(al, bh))


def vmem():
    return pl.BlockSpec(memory_space=pltpu.VMEM)


def smem():
    return pl.BlockSpec(memory_space=pltpu.SMEM)


def hbm():
    return pl.BlockSpec(memory_space=pltpu.HBM)


def params(mib):
    return pltpu.CompilerParams(vmem_limit_bytes=mib * MIB)


def pack_body(info, ids_hbm, pts_hbm, res_hbm, out_ref, tab_ref, ids_ref, pts_ref, res_ref, sems, *, n_plane, n_col):
    me = info[2]
    rows = pts_ref.shape[0]
    ids_in = pltpu.make_async_copy(ids_hbm, ids_ref, sems.at[0])
    pts_in = pltpu.make_async_copy(pts_hbm, pts_ref, sems.at[1])
    res_in = pltpu.make_async_copy(res_hbm, res_ref, sems.at[2])
    ids_in.start()
    pts_in.start()
    res_in.start()
    ids_in.wait()
    ids = ids_ref[...]
    n = ids.shape[1]
    eye = iota((n, n), 0) == iota((n, n), 1)
    ids_col = jnp.sum(jnp.where(eye, jnp.broadcast_to(ids, (n, n)), 0), axis=1, keepdims=True)
    owner = ids // rows
    column = ids // (rows * n_col)
    less = jnp.broadcast_to(ids_col, (n, n)) < ids
    rank = jnp.sum(jnp.where(less & (ids_col >= column * (rows * n_col)), 1, 0), axis=0, keepdims=True)
    slot = jnp.sum(jnp.where(less & (ids_col >= owner * rows), 1, 0), axis=0, keepdims=True)
    planes = COL_CAP * n_plane
    straight = column * COL_CAP + rank
    turned = planes - COL_CAP - column * COL_CAP + rank
    here = jnp.where(info[0] == 0, straight, turned)
    there = jnp.where(info[0] == 0, turned, straight)
    tab_ref[...] = jnp.concatenate([ids, rank, slot, here, there, jnp.zeros((3, n), I32)], axis=0)
    mine = owner == me
    lane = iota((8, rows), 1)
    sub = iota((8, rows), 0)
    take = jnp.zeros((8, rows), F32)
    for k in range(CAP):
        at = jnp.max(jnp.where(mine & (slot == k), ids - me * rows, -1), axis=1, keepdims=True)
        take = jnp.where((sub == k) & (lane == at), 1.0, take)
    take = take.astype(BF)
    pts_in.wait()
    picked = dot(take, pts_ref[...]).astype(BF)
    res_in.wait()
    res = res_ref[...]
    hi = res.astype(BF)
    low = (res - hi.astype(F32)).astype(BF)
    classes = res.shape[0]
    pad = jnp.zeros((8, CLASS_PAD - classes), F32)
    parts = [jnp.concatenate([dot(take, v, NT), pad], axis=1).astype(BF) for v in (hi, low)]
    half = pts_ref.shape[1] // 2
    chalf = CLASS_PAD // 2
    for core in range(2):
        row = [picked[:CAP, core * half : (core + 1) * half]]
        row += [v[:CAP, core * CLASS_STEP : core * CLASS_STEP + chalf] for v in parts]
        row = jnp.concatenate(row, axis=1).astype(F32)
        w = row.shape[1] // SPLIT
        block = jnp.concatenate([row[:, q * w : (q + 1) * w] for q in range(SPLIT)], axis=0).astype(BF)
        for z in range(n_col // 2):
            out_ref[2 * z + core] = block


def pack(info, ids, points, res_t, n_plane, n_col):
    width = points.shape[1] // 2 + CLASS_PAD
    n = ids.shape[1]
    return pl.pallas_call(
        functools.partial(pack_body, n_plane=n_plane, n_col=n_col),
        out_shape=(
            jax.ShapeDtypeStruct((n_col, CAP * SPLIT, width // SPLIT), BF),
            jax.ShapeDtypeStruct((8, n), I32),
        ),
        in_specs=[smem(), hbm(), hbm(), hbm()],
        out_specs=(vmem(), vmem()),
        scratch_shapes=[
            pltpu.VMEM(ids.shape, I32),
            pltpu.VMEM(points.shape, BF),
            pltpu.VMEM(res_t.shape, F32),
            pltpu.SemaphoreType.DMA((3,)),
        ],
        compiler_params=params(60),
    )(info, ids, points, res_t)


def table(tab_ref):
    return tab_ref[0:1, :], tab_ref[1:2, :], tab_ref[2:3, :]


def encode(res):
    top = jnp.max(jnp.abs(res), axis=1, keepdims=True)
    power = jnp.floor(jnp.log2(jnp.maximum(top, 1e-30))) + 1.0
    code = jnp.floor(res * (FRACTION / jnp.exp2(power)) + 0.5).astype(I32)
    code = jnp.where(iota(res.shape, 1) == SCALE_LANE, power.astype(I32) * 256, code)
    low = code & 255
    half = res.shape[1] // 2
    pair = (low[:, :half] | (low[:, half:] << 8)) - 32768
    return jnp.concatenate([code >> 8, pair], axis=1).astype(jnp.int16)


def decode(words):
    words = words.astype(I32)
    n = words.shape[1] * 2 // 3
    high = words[:, :n]
    pair = words[:, n:] + 32768
    low = jnp.concatenate([pair & 255, pair >> 8], axis=1)
    unit = jnp.exp2(high[:, SCALE_LANE : SCALE_LANE + 1].astype(F32)) * (1.0 / FRACTION)
    return (high * 256 + low).astype(F32) * unit


def compact_body(info, tab_ref, in_ref, pts_ref, res_ref, *, rows, n_col):
    plane = info[1]
    ids, rank, slot = table(tab_ref)
    n = ids.shape[1]
    owner = ids // rows
    column = ids // (rows * n_col)
    wide = in_ref.shape[0]
    sel_rank = (iota((COL_CAP, n), 0) == rank) & (column == plane)
    at = iota((wide, n), 0)
    group = CAP * SPLIT
    sel_slot = (at // group == owner - column * n_col) & (at % CAP == slot)
    pick = dot(sel_rank.astype(F32).astype(BF), sel_slot.astype(F32).astype(BF), NT)
    part = (iota((COL_CAP, wide), 1) // CAP) % SPLIT
    data = in_ref[...]
    whole = [dot(jnp.where(part == q, pick, 0.0).astype(BF), data) for q in range(SPLIT)]
    whole = jnp.concatenate(whole, axis=1)
    half = pts_ref.shape[2]
    pts = whole[:, :half].astype(BF)
    chalf = CLASS_PAD // 2
    res = encode(whole[:, half : half + chalf] + whole[:, half + chalf :])
    for p in range(pts_ref.shape[0]):
        pts_ref[p] = pts
        res_ref[p] = res


def compact(info, tab, data, rows, half, n_plane, n_col):
    return pl.pallas_call(
        functools.partial(compact_body, rows=rows, n_col=n_col),
        out_shape=(
            jax.ShapeDtypeStruct((n_plane, COL_CAP, half), BF),
            jax.ShapeDtypeStruct((n_plane, COL_CAP, CLASS_PAD * 3 // 4), jnp.int16),
        ),
        in_specs=[smem(), vmem(), vmem()],
        out_specs=(vmem(), vmem()),
        compiler_params=params(16),
    )(info, tab, data)


def place_matrix(tab_ref, wide, row=3):
    at = tab_ref[row : row + 1, :]
    return (iota((wide, at.shape[1]), 0) == at).astype(F32).astype(BF)


def order_body(tab_ref, in_ref, out_ref):
    out_ref[...] = dot(place_matrix(tab_ref, in_ref.shape[0]), in_ref[...], TN).astype(BF)


def order(tab, data):
    return pl.pallas_call(
        order_body,
        out_shape=jax.ShapeDtypeStruct((tab.shape[1], data.shape[1]), BF),
        in_specs=[vmem(), vmem()],
        out_specs=vmem(),
        compiler_params=params(10),
    )(tab, data)


def first_half_body(info, pts_ref, own_ref, cross_ref, p_cross_ref, psq_ref, p_oth_ref, *, half):
    core = info[0]
    own = own_ref[...]
    cross_ref[...] = dot(own, own, NT)
    p_own = pts_ref[:, pl.ds(pl.multiple_of(core * half, half), half)]
    p_oth = pts_ref[:, pl.ds(pl.multiple_of((1 - core) * half, half), half)]
    p_cross_ref[...] = dot(p_own, own, NT)
    p_oth_ref[...] = p_oth
    a = p_own.astype(F32)
    b = p_oth.astype(F32)
    psq_ref[...] = jnp.sum(a * a, axis=1, keepdims=True) + jnp.sum(b * b, axis=1, keepdims=True)


def first_half(info, points, own):
    n, half = own.shape
    rows = points.shape[0]
    return pl.pallas_call(
        functools.partial(first_half_body, half=half),
        out_shape=(
            jax.ShapeDtypeStruct((n, n), F32),
            jax.ShapeDtypeStruct((rows, n), F32),
            jax.ShapeDtypeStruct((rows, 1), F32),
            jax.ShapeDtypeStruct((rows, half), BF),
        ),
        in_specs=[smem(), vmem(), vmem()],
        out_specs=(vmem(),) * 4,
        compiler_params=params(12),
        cost_estimate=pl.CostEstimate(flops=10**6, bytes_accessed=10**6, transcendentals=0),
    )(info, points, own)


def inverse_body(info, tab_ref, p_oth_ref, oth_ref, cross_ref, p_cross_ref, psq_ref, hi_ref, lo_ref, g_ref, m_ref, gh_ref, gl_ref, x_ref, *, share):
    n = oth_ref.shape[0]
    rows = p_cross_ref.shape[0]
    me, share_at = info[2], info[3]
    oth = oth_ref[...]
    cross = cross_ref[...] + dot(oth, oth, NT)
    eye = iota((n, n), 0) == iota((n, n), 1)
    diag = jnp.where(eye, cross, 0.0)
    sq_row = jnp.sum(diag, axis=0, keepdims=True)
    sq_col = jnp.sum(diag, axis=1, keepdims=True)
    gram = jnp.exp(-GAMMA * (sq_col + sq_row - 2.0 * cross)) + jnp.where(eye, RIDGE, 0.0)
    g_ref[...] = gram
    gh, gl = two_parts(gram)
    gh_ref[...] = gh
    gl_ref[...] = gl
    p_cross = p_cross_ref[...] + dot(p_oth_ref[...], oth, NT)
    p_kern = jnp.exp(-GAMMA * (psq_ref[...] + sq_row - 2.0 * p_cross))
    point_id = me * rows + iota((rows, n), 0)
    m_ref[pl.ds(0, rows), :] = p_kern + jnp.where(point_id == table(tab_ref)[0], RIDGE, 0.0)
    m_ref[pl.ds(rows, share), :] = jnp.where(share_at + iota((share, n), 0) == iota((share, n), 1), 1.0, 0.0)
    lo = 0.499
    gram = g_ref[...]
    v_col = jnp.sum(gram, axis=1, keepdims=True)
    v_row = jnp.sum(gram, axis=0, keepdims=True)
    hi = jnp.max(jnp.sum(gram * v_col, axis=0, keepdims=True) / v_row) * 1.001
    s = 2.0 / (lo + hi)
    x_ref[...] = jnp.where(eye, 2.0 * s, 0.0) - (s * s) * gram
    d = (hi - lo) / (hi + lo)

    def refine(resid):
        x = x_ref[...] * (2.0 / (2.0 - resid))
        xh, xl = two_parts(x)
        r = (jnp.where(eye, 1.0, 0.0) - mm3((gh_ref[...], gl_ref[...]), (xh, xl))).astype(BF)
        x_ref[...] = x + (dot(xh, r) + dot(xl, r))
        after = resid / (2.0 - resid)
        return after * after

    lax.while_loop(lambda resid: resid > 5e-4, refine, d * d)
    xs = two_parts(x_ref[...])
    m = m_ref[...]
    w = mm3(two_parts(m), xs)
    e = m - dot(w, g_ref[...], NN, HI)
    w = w + mm3(two_parts(e), xs)
    wh, wl = two_parts(w)
    hi_ref[...] = wh
    lo_ref[...] = wl


def inverse(info, tab, p_oth, oth, cross, p_cross, psq, share):
    n = oth.shape[0]
    rows = p_oth.shape[0]
    out = jax.ShapeDtypeStruct((rows + share, n), BF)
    return pl.pallas_call(
        functools.partial(inverse_body, share=share),
        out_shape=(out, out),
        in_specs=[smem()] + [vmem()] * 6,
        out_specs=(vmem(), vmem()),
        scratch_shapes=[
            pltpu.VMEM((n, n), F32),
            pltpu.VMEM((rows + share, n), F32),
            pltpu.VMEM((n, n), BF),
            pltpu.VMEM((n, n), BF),
            pltpu.VMEM((n, n), F32),
        ],
        compiler_params=params(18),
        cost_estimate=pl.CostEstimate(flops=10**6, bytes_accessed=10**6, transcendentals=0),
    )(info, tab, p_oth, oth, cross, p_cross, psq)


def apply_weights(hi, lo, res_ref):
    return mm3((hi, lo), two_parts(decode(res_ref[...])))


def update_own_body(tab_ref, wh_ref, wl_ref, res_ref, hi_ref, lo_ref, ch_ref):
    wide = res_ref.shape[0]
    here = place_matrix(tab_ref, wide)
    hi = dot(wh_ref[...], here, NT).astype(BF)
    lo = dot(wl_ref[...], here, NT).astype(BF)
    ch_ref[...] = apply_weights(hi, lo, res_ref)
    there = place_matrix(tab_ref, wide, 4)
    hi_ref[...] = dot(wh_ref[...], there, NT).astype(BF)
    lo_ref[...] = dot(wl_ref[...], there, NT).astype(BF)


def update_own(tab, wh, wl, res):
    m = wh.shape[0]
    wide = res.shape[0]
    out = jax.ShapeDtypeStruct((m, wide), BF)
    return pl.pallas_call(
        update_own_body,
        out_shape=(out, out, jax.ShapeDtypeStruct((m, CLASS_PAD // 2), F32)),
        in_specs=[vmem()] * 4,
        out_specs=(vmem(),) * 3,
        compiler_params=params(10),
        cost_estimate=pl.CostEstimate(flops=2 * 10**9, bytes_accessed=4 * 10**6, transcendentals=0),
    )(tab, wh, wl, res)


def update_other_body(info, hi_ref, lo_ref, res_ref, ch_ref, res_t_ref, out_ref, share_ref):
    core = info[0]
    classes, rows = res_t_ref.shape
    skip = 2 * CLASS_SPAN - classes
    mine = ch_ref[...]
    theirs = apply_weights(hi_ref[...], lo_ref[...], res_ref)
    low = jnp.where(core == 0, mine, theirs)
    high = jnp.where(core == 0, theirs, mine)
    share_ref[...] = jnp.concatenate([low[rows:, :CLASS_SPAN], high[rows:, skip:CLASS_SPAN]], axis=1)
    out_ref[:CLASS_SPAN, :] = res_t_ref[:CLASS_SPAN, :] - low[:rows].T[:CLASS_SPAN]
    out_ref[CLASS_SPAN:, :] = res_t_ref[CLASS_SPAN:, :] - high[:rows].T[skip:CLASS_SPAN]


def update_other(info, hi, lo, res, change, res_t, share):
    classes, rows = res_t.shape
    return pl.pallas_call(
        update_other_body,
        out_shape=(jax.ShapeDtypeStruct((classes, rows), F32), jax.ShapeDtypeStruct((share, classes), F32)),
        in_specs=[smem()] + [vmem()] * 5,
        out_specs=(vmem(), vmem()),
        compiler_params=params(16),
    )(info, hi, lo, res, change, res_t)


def plane_groups():
    groups = []
    for place in range(32):
        members = [p * 32 + place for p in range(16)]
        groups.append(members if place % 2 == 0 else members[::-1])
    return groups


def over_plane(value):
    return lax.all_to_all(value, EVERY, 0, 0, axis_index_groups=plane_groups(), tiled=True)


def on_device(points, residual, block_ids):
    rows, feats = points.shape
    block = block_ids.shape[0]
    n_plane = lax.axis_size(PLANE)
    n_col = lax.axis_size(COLUMN)
    n_gy = lax.axis_size("zl") * lax.axis_size("c")
    plane = lax.axis_index(PLANE)
    place = lax.axis_index(COLUMN)
    share = block // n_gy
    half = feats // 2
    wide = n_plane * COL_CAP
    info = jnp.stack([lax.axis_index("c"), plane, plane * n_col + place, (place % n_gy) * share]).astype(I32)
    ids = block_ids.reshape(1, block)
    res_t = residual.T
    swap = [(0, 1), (1, 0)]

    packed, tab = pack(info, ids, points, res_t, n_plane, n_col)
    col_rows = lax.all_to_all(packed, COLUMN, 0, 0, tiled=True)
    col_rows = col_rows.reshape(n_col * CAP * SPLIT, col_rows.shape[2])
    pts_out, res_out = compact(info, tab, col_rows, rows, half, n_plane, n_col)
    all_pts = over_plane(pts_out).reshape(wide, half)
    all_res = over_plane(res_out).reshape(wide, CLASS_PAD * 3 // 4)
    own = order(tab, all_pts)
    other = lax.ppermute(own, "c", swap)
    cross, p_cross, psq, p_oth = first_half(info, points, own)
    wh, wl = inverse(info, tab, p_oth, other, cross, p_cross, psq, share)
    all_res, wh = lax.optimization_barrier((all_res, wh))
    other_res = lax.ppermute(all_res, "c", swap)
    hi, lo, change = update_own(tab, wh, wl, all_res)
    out_t, step_share = update_other(info, hi, lo, other_res, change, res_t, share)
    return (out_t.T, step_share)


def solution(mesh):
    fine = Mesh(mesh.devices.reshape(4, 4, 2, 8, 2), EVERY)
    return jax.shard_map(
        on_device,
        mesh=fine,
        in_specs=(P(EVERY, None), P(EVERY, None), P()),
        out_specs=(P(EVERY, None), P(("zl", "c"), None)),
        check_vma=False,
    )
```

```python
import functools

import jax
import jax.numpy as jnp
from jax import lax
from jax.experimental import pallas as pl
from jax.experimental.pallas import tpu as pltpu
from jax.sharding import Mesh
from jax.sharding import PartitionSpec as P

F32 = jnp.float32
BF = jnp.bfloat16
I32 = jnp.int32
HI = lax.Precision.HIGHEST
NN = (((1,), (0,)), ((), ()))
NT = (((1,), (1,)), ((), ()))
TN = (((0,), (0,)), ((), ()))

GAMMA = 0.125
RIDGE = 0.5
PLANE = ("y", "x")
COLUMN = ("zh", "zl", "c")
EVERY = PLANE + COLUMN
CAP = 2
COL_CAP = 48
CLASS_PAD = 1024
SPLIT = 4
CLASS_STEP = 496
CLASS_SPAN = 504
SCALE_LANE = 511
FRACTION = 2.0**22
MIB = 1024 * 1024


def dot(a, b, dn=NN, prec=None):
    return lax.dot_general(a, b, dn, preferred_element_type=F32, precision=prec)


def iota(shape, axis):
    return lax.broadcasted_iota(I32, shape, axis)


def two_parts(v):
    hi = v.astype(BF)
    return hi, (v - hi.astype(F32)).astype(BF)


def mm3(a, b):
    ah, al = a
    bh, bl = b
    return dot(ah, bh) + (dot(ah, bl) + dot(al, bh))


def vmem():
    return pl.BlockSpec(memory_space=pltpu.VMEM)


def smem():
    return pl.BlockSpec(memory_space=pltpu.SMEM)


def hbm():
    return pl.BlockSpec(memory_space=pltpu.HBM)


def params(mib):
    return pltpu.CompilerParams(vmem_limit_bytes=mib * MIB)


def pack_body(info, ids_hbm, pts_hbm, res_hbm, out_ref, tab_ref, ids_ref, pts_ref, res_ref, sems, *, n_plane, n_col):
    me = info[2]
    rows = pts_ref.shape[0]
    ids_in = pltpu.make_async_copy(ids_hbm, ids_ref, sems.at[0])
    pts_in = pltpu.make_async_copy(pts_hbm, pts_ref, sems.at[1])
    res_in = pltpu.make_async_copy(res_hbm, res_ref, sems.at[2])
    ids_in.start()
    pts_in.start()
    res_in.start()
    ids_in.wait()
    ids = ids_ref[...]
    n = ids.shape[1]
    eye = iota((n, n), 0) == iota((n, n), 1)
    ids_col = jnp.sum(jnp.where(eye, jnp.broadcast_to(ids, (n, n)), 0), axis=1, keepdims=True)
    owner = ids // rows
    column = ids // (rows * n_col)
    less = jnp.broadcast_to(ids_col, (n, n)) < ids
    rank = jnp.sum(jnp.where(less & (ids_col >= column * (rows * n_col)), 1, 0), axis=0, keepdims=True)
    slot = jnp.sum(jnp.where(less & (ids_col >= owner * rows), 1, 0), axis=0, keepdims=True)
    planes = COL_CAP * n_plane
    straight = column * COL_CAP + rank
    turned = planes - COL_CAP - column * COL_CAP + rank
    here = jnp.where(info[0] == 0, straight, turned)
    there = jnp.where(info[0] == 0, turned, straight)
    tab_ref[...] = jnp.concatenate([ids, rank, slot, here, there, jnp.zeros((3, n), I32)], axis=0)
    mine = owner == me
    lane = iota((8, rows), 1)
    sub = iota((8, rows), 0)
    take = jnp.zeros((8, rows), F32)
    for k in range(CAP):
        at = jnp.max(jnp.where(mine & (slot == k), ids - me * rows, -1), axis=1, keepdims=True)
        take = jnp.where((sub == k) & (lane == at), 1.0, take)
    take = take.astype(BF)
    pts_in.wait()
    picked = dot(take, pts_ref[...]).astype(BF)
    res_in.wait()
    res = res_ref[...]
    hi = res.astype(BF)
    low = (res - hi.astype(F32)).astype(BF)
    classes = res.shape[0]
    pad = jnp.zeros((8, CLASS_PAD - classes), F32)
    parts = [jnp.concatenate([dot(take, v, NT), pad], axis=1).astype(BF) for v in (hi, low)]
    half = pts_ref.shape[1] // 2
    chalf = CLASS_PAD // 2
    for core in range(2):
        row = [picked[:CAP, core * half : (core + 1) * half]]
        row += [v[:CAP, core * CLASS_STEP : core * CLASS_STEP + chalf] for v in parts]
        row = jnp.concatenate(row, axis=1).astype(F32)
        w = row.shape[1] // SPLIT
        block = jnp.concatenate([row[:, q * w : (q + 1) * w] for q in range(SPLIT)], axis=0).astype(BF)
        for z in range(n_col // 2):
            out_ref[2 * z + core] = block


def pack(info, ids, points, res_t, n_plane, n_col):
    width = points.shape[1] // 2 + CLASS_PAD
    n = ids.shape[1]
    return pl.pallas_call(
        functools.partial(pack_body, n_plane=n_plane, n_col=n_col),
        out_shape=(
            jax.ShapeDtypeStruct((n_col, CAP * SPLIT, width // SPLIT), BF),
            jax.ShapeDtypeStruct((8, n), I32),
        ),
        in_specs=[smem(), hbm(), hbm(), hbm()],
        out_specs=(vmem(), vmem()),
        scratch_shapes=[
            pltpu.VMEM(ids.shape, I32),
            pltpu.VMEM(points.shape, BF),
            pltpu.VMEM(res_t.shape, F32),
            pltpu.SemaphoreType.DMA((3,)),
        ],
        compiler_params=params(60),
    )(info, ids, points, res_t)


def table(tab_ref):
    return tab_ref[0:1, :], tab_ref[1:2, :], tab_ref[2:3, :]


def encode(res):
    top = jnp.max(jnp.abs(res), axis=1, keepdims=True)
    power = jnp.floor(jnp.log2(jnp.maximum(top, 1e-30))) + 1.0
    code = jnp.floor(res * (FRACTION / jnp.exp2(power)) + 0.5).astype(I32)
    code = jnp.where(iota(res.shape, 1) == SCALE_LANE, power.astype(I32) * 256, code)
    low = code & 255
    half = res.shape[1] // 2
    pair = (low[:, :half] | (low[:, half:] << 8)) - 32768
    return jnp.concatenate([code >> 8, pair], axis=1).astype(jnp.int16)


def decode(words):
    words = words.astype(I32)
    n = words.shape[1] * 2 // 3
    high = words[:, :n]
    pair = words[:, n:] + 32768
    low = jnp.concatenate([pair & 255, pair >> 8], axis=1)
    unit = jnp.exp2(high[:, SCALE_LANE : SCALE_LANE + 1].astype(F32)) * (1.0 / FRACTION)
    return (high * 256 + low).astype(F32) * unit


def compact_body(info, tab_ref, in_ref, pts_ref, res_ref, *, rows, n_col):
    plane = info[1]
    ids, rank, slot = table(tab_ref)
    n = ids.shape[1]
    owner = ids // rows
    column = ids // (rows * n_col)
    wide = in_ref.shape[0]
    sel_rank = (iota((COL_CAP, n), 0) == rank) & (column == plane)
    at = iota((wide, n), 0)
    group = CAP * SPLIT
    sel_slot = (at // group == owner - column * n_col) & (at % CAP == slot)
    pick = dot(sel_rank.astype(F32).astype(BF), sel_slot.astype(F32).astype(BF), NT)
    part = (iota((COL_CAP, wide), 1) // CAP) % SPLIT
    data = in_ref[...]
    whole = [dot(jnp.where(part == q, pick, 0.0).astype(BF), data) for q in range(SPLIT)]
    whole = jnp.concatenate(whole, axis=1)
    half = pts_ref.shape[2]
    pts = whole[:, :half].astype(BF)
    chalf = CLASS_PAD // 2
    res = encode(whole[:, half : half + chalf] + whole[:, half + chalf :])
    for p in range(pts_ref.shape[0]):
        pts_ref[p] = pts
        res_ref[p] = res


def compact(info, tab, data, rows, half, n_plane, n_col):
    return pl.pallas_call(
        functools.partial(compact_body, rows=rows, n_col=n_col),
        out_shape=(
            jax.ShapeDtypeStruct((n_plane, COL_CAP, half), BF),
            jax.ShapeDtypeStruct((n_plane, COL_CAP, CLASS_PAD * 3 // 4), jnp.int16),
        ),
        in_specs=[smem(), vmem(), vmem()],
        out_specs=(vmem(), vmem()),
        compiler_params=params(16),
    )(info, tab, data)


def place_matrix(tab_ref, wide, row=3):
    at = tab_ref[row : row + 1, :]
    return (iota((wide, at.shape[1]), 0) == at).astype(F32).astype(BF)


def order_body(tab_ref, in_ref, out_ref):
    out_ref[...] = dot(place_matrix(tab_ref, in_ref.shape[0]), in_ref[...], TN).astype(BF)


def order(tab, data):
    return pl.pallas_call(
        order_body,
        out_shape=jax.ShapeDtypeStruct((tab.shape[1], data.shape[1]), BF),
        in_specs=[vmem(), vmem()],
        out_specs=vmem(),
        compiler_params=params(10),
    )(tab, data)


def first_half_body(info, pts_ref, own_ref, cross_ref, p_cross_ref, psq_ref, p_oth_ref, *, half):
    core = info[0]
    own = own_ref[...]
    cross_ref[...] = dot(own, own, NT)
    p_own = pts_ref[:, pl.ds(pl.multiple_of(core * half, half), half)]
    p_oth = pts_ref[:, pl.ds(pl.multiple_of((1 - core) * half, half), half)]
    p_cross_ref[...] = dot(p_own, own, NT)
    p_oth_ref[...] = p_oth
    a = p_own.astype(F32)
    b = p_oth.astype(F32)
    psq_ref[...] = jnp.sum(a * a, axis=1, keepdims=True) + jnp.sum(b * b, axis=1, keepdims=True)


def first_half(info, points, own):
    n, half = own.shape
    rows = points.shape[0]
    return pl.pallas_call(
        functools.partial(first_half_body, half=half),
        out_shape=(
            jax.ShapeDtypeStruct((n, n), F32),
            jax.ShapeDtypeStruct((rows, n), F32),
            jax.ShapeDtypeStruct((rows, 1), F32),
            jax.ShapeDtypeStruct((rows, half), BF),
        ),
        in_specs=[smem(), vmem(), vmem()],
        out_specs=(vmem(),) * 4,
        compiler_params=params(12),
        cost_estimate=pl.CostEstimate(flops=10**6, bytes_accessed=10**6, transcendentals=0),
    )(info, points, own)


def inverse_body(info, tab_ref, p_oth_ref, oth_ref, cross_ref, p_cross_ref, psq_ref, hi_ref, lo_ref, g_ref, m_ref, gh_ref, gl_ref, x_ref, *, share):
    n = oth_ref.shape[0]
    rows = p_cross_ref.shape[0]
    me, share_at = info[2], info[3]
    oth = oth_ref[...]
    cross = cross_ref[...] + dot(oth, oth, NT)
    eye = iota((n, n), 0) == iota((n, n), 1)
    diag = jnp.where(eye, cross, 0.0)
    sq_row = jnp.sum(diag, axis=0, keepdims=True)
    sq_col = jnp.sum(diag, axis=1, keepdims=True)
    gram = jnp.exp(-GAMMA * (sq_col + sq_row - 2.0 * cross)) + jnp.where(eye, RIDGE, 0.0)
    g_ref[...] = gram
    gh, gl = two_parts(gram)
    gh_ref[...] = gh
    gl_ref[...] = gl
    p_cross = p_cross_ref[...] + dot(p_oth_ref[...], oth, NT)
    p_kern = jnp.exp(-GAMMA * (psq_ref[...] + sq_row - 2.0 * p_cross))
    point_id = me * rows + iota((rows, n), 0)
    m_ref[pl.ds(0, rows), :] = p_kern + jnp.where(point_id == table(tab_ref)[0], RIDGE, 0.0)
    m_ref[pl.ds(rows, share), :] = jnp.where(share_at + iota((share, n), 0) == iota((share, n), 1), 1.0, 0.0)
    lo = 0.499
    gram = g_ref[...]
    v_col = jnp.sum(gram, axis=1, keepdims=True)
    v_row = jnp.sum(gram, axis=0, keepdims=True)
    hi = jnp.max(jnp.sum(gram * v_col, axis=0, keepdims=True) / v_row) * 1.001
    s = 2.0 / (lo + hi)
    x_ref[...] = jnp.where(eye, 2.0 * s, 0.0) - (s * s) * gram
    d = (hi - lo) / (hi + lo)

    def refine(resid, whole):
        x = x_ref[...] * (2.0 / (2.0 - resid))
        xh, xl = two_parts(x)
        gh = gh_ref[...]
        gx = dot(gh, xh) + (dot(gh, xl) + dot(gl_ref[...], xh) if whole else dot(gh, xl))
        r = (jnp.where(eye, 1.0, 0.0) - gx).astype(BF)
        x_ref[...] = x + (dot(xh, r) + dot(xl, r))
        after = resid / (2.0 - resid)
        return after * after

    resid = lax.while_loop(lambda v: v > 0.5, functools.partial(refine, whole=False), d * d)
    lax.while_loop(lambda v: v > 0.02, functools.partial(refine, whole=True), resid)
    xh, xl = two_parts(x_ref[...])
    m = m_ref[...]
    w = mm3(two_parts(m), (xh, xl))
    e = (m - mm3(two_parts(w), (gh_ref[...], gl_ref[...]))).astype(BF)
    w = w + (dot(e, xh) + dot(e, xl))
    e = (m - dot(w, g_ref[...], NN, HI)).astype(BF)
    w = w + (dot(e, xh) + dot(e, xl))
    wh, wl = two_parts(w)
    hi_ref[...] = wh
    lo_ref[...] = wl


def inverse(info, tab, p_oth, oth, cross, p_cross, psq, share):
    n = oth.shape[0]
    rows = p_oth.shape[0]
    out = jax.ShapeDtypeStruct((rows + share, n), BF)
    return pl.pallas_call(
        functools.partial(inverse_body, share=share),
        out_shape=(out, out),
        in_specs=[smem()] + [vmem()] * 6,
        out_specs=(vmem(), vmem()),
        scratch_shapes=[
            pltpu.VMEM((n, n), F32),
            pltpu.VMEM((rows + share, n), F32),
            pltpu.VMEM((n, n), BF),
            pltpu.VMEM((n, n), BF),
            pltpu.VMEM((n, n), F32),
        ],
        compiler_params=params(18),
        cost_estimate=pl.CostEstimate(flops=10**6, bytes_accessed=10**6, transcendentals=0),
    )(info, tab, p_oth, oth, cross, p_cross, psq)


def apply_weights(hi, lo, res_ref):
    return mm3((hi, lo), two_parts(decode(res_ref[...])))


def update_own_body(tab_ref, wh_ref, wl_ref, res_ref, hi_ref, lo_ref, ch_ref):
    wide = res_ref.shape[0]
    here = place_matrix(tab_ref, wide)
    hi = dot(wh_ref[...], here, NT).astype(BF)
    lo = dot(wl_ref[...], here, NT).astype(BF)
    ch_ref[...] = apply_weights(hi, lo, res_ref)
    there = place_matrix(tab_ref, wide, 4)
    hi_ref[...] = dot(wh_ref[...], there, NT).astype(BF)
    lo_ref[...] = dot(wl_ref[...], there, NT).astype(BF)


def update_own(tab, wh, wl, res):
    m = wh.shape[0]
    wide = res.shape[0]
    out = jax.ShapeDtypeStruct((m, wide), BF)
    return pl.pallas_call(
        update_own_body,
        out_shape=(out, out, jax.ShapeDtypeStruct((m, CLASS_PAD // 2), F32)),
        in_specs=[vmem()] * 4,
        out_specs=(vmem(),) * 3,
        compiler_params=params(10),
        cost_estimate=pl.CostEstimate(flops=2 * 10**9, bytes_accessed=4 * 10**6, transcendentals=0),
    )(tab, wh, wl, res)


def update_other_body(info, hi_ref, lo_ref, res_ref, ch_ref, res_t_ref, out_ref, share_ref):
    core = info[0]
    classes, rows = res_t_ref.shape
    skip = 2 * CLASS_SPAN - classes
    mine = ch_ref[...]
    theirs = apply_weights(hi_ref[...], lo_ref[...], res_ref)
    low = jnp.where(core == 0, mine, theirs)
    high = jnp.where(core == 0, theirs, mine)
    share_ref[...] = jnp.concatenate([low[rows:, :CLASS_SPAN], high[rows:, skip:CLASS_SPAN]], axis=1)
    out_ref[:CLASS_SPAN, :] = res_t_ref[:CLASS_SPAN, :] - low[:rows].T[:CLASS_SPAN]
    out_ref[CLASS_SPAN:, :] = res_t_ref[CLASS_SPAN:, :] - high[:rows].T[skip:CLASS_SPAN]


def update_other(info, hi, lo, res, change, res_t, share):
    classes, rows = res_t.shape
    return pl.pallas_call(
        update_other_body,
        out_shape=(jax.ShapeDtypeStruct((classes, rows), F32), jax.ShapeDtypeStruct((share, classes), F32)),
        in_specs=[smem()] + [vmem()] * 5,
        out_specs=(vmem(), vmem()),
        compiler_params=params(16),
    )(info, hi, lo, res, change, res_t)


def plane_groups():
    groups = []
    for place in range(32):
        members = [p * 32 + place for p in range(16)]
        groups.append(members if place % 2 == 0 else members[::-1])
    return groups


def over_plane(value):
    return lax.all_to_all(value, EVERY, 0, 0, axis_index_groups=plane_groups(), tiled=True)


def on_device(points, residual, block_ids):
    rows, feats = points.shape
    block = block_ids.shape[0]
    n_plane = lax.axis_size(PLANE)
    n_col = lax.axis_size(COLUMN)
    n_gy = lax.axis_size("zl") * lax.axis_size("c")
    plane = lax.axis_index(PLANE)
    place = lax.axis_index(COLUMN)
    share = block // n_gy
    half = feats // 2
    wide = n_plane * COL_CAP
    info = jnp.stack([lax.axis_index("c"), plane, plane * n_col + place, (place % n_gy) * share]).astype(I32)
    ids = block_ids.reshape(1, block)
    res_t = residual.T
    swap = [(0, 1), (1, 0)]

    packed, tab = pack(info, ids, points, res_t, n_plane, n_col)
    col_rows = lax.all_to_all(packed, COLUMN, 0, 0, tiled=True)
    col_rows = col_rows.reshape(n_col * CAP * SPLIT, col_rows.shape[2])
    pts_out, res_out = compact(info, tab, col_rows, rows, half, n_plane, n_col)
    all_pts = over_plane(pts_out).reshape(wide, half)
    all_res = over_plane(res_out).reshape(wide, CLASS_PAD * 3 // 4)
    own = order(tab, all_pts)
    other = lax.ppermute(own, "c", swap)
    cross, p_cross, psq, p_oth = first_half(info, points, own)
    wh, wl = inverse(info, tab, p_oth, other, cross, p_cross, psq, share)
    all_res, wh = lax.optimization_barrier((all_res, wh))
    other_res = lax.ppermute(all_res, "c", swap)
    hi, lo, change = update_own(tab, wh, wl, all_res)
    out_t, step_share = update_other(info, hi, lo, other_res, change, res_t, share)
    return (out_t.T, step_share)


def solution(mesh):
    fine = Mesh(mesh.devices.reshape(4, 4, 2, 8, 2), EVERY)
    return jax.shard_map(
        on_device,
        mesh=fine,
        in_specs=(P(EVERY, None), P(EVERY, None), P()),
        out_specs=(P(EVERY, None), P(("zl", "c"), None)),
        check_vma=False,
    )
```

```python
import functools

import jax
import jax.numpy as jnp
from jax import lax
from jax.experimental import pallas as pl
from jax.experimental.pallas import tpu as pltpu
from jax.sharding import Mesh
from jax.sharding import PartitionSpec as P

F32 = jnp.float32
BF = jnp.bfloat16
I32 = jnp.int32
HI = lax.Precision.HIGHEST
NN = (((1,), (0,)), ((), ()))
NT = (((1,), (1,)), ((), ()))
TN = (((0,), (0,)), ((), ()))

GAMMA = 0.125
RIDGE = 0.5
PLANE = ("y", "x")
COLUMN = ("zh", "zl", "c")
EVERY = PLANE + COLUMN
CAP = 2
COL_CAP = 48
CLASS_PAD = 1024
SPLIT = 4
CLASS_STEP = 496
CLASS_SPAN = 504
SCALE_LANE = 511
FRACTION = 500000.0
CODED = 640
MIB = 1024 * 1024


def dot(a, b, dn=NN, prec=None):
    return lax.dot_general(a, b, dn, preferred_element_type=F32, precision=prec)


def iota(shape, axis):
    return lax.broadcasted_iota(I32, shape, axis)


def two_parts(v):
    hi = v.astype(BF)
    return hi, (v - hi.astype(F32)).astype(BF)


def mm3(a, b):
    ah, al = a
    bh, bl = b
    return dot(ah, bh) + (dot(ah, bl) + dot(al, bh))


def vmem():
    return pl.BlockSpec(memory_space=pltpu.VMEM)


def smem():
    return pl.BlockSpec(memory_space=pltpu.SMEM)


def hbm():
    return pl.BlockSpec(memory_space=pltpu.HBM)


def params(mib):
    return pltpu.CompilerParams(vmem_limit_bytes=mib * MIB)


def pack_body(info, ids_hbm, pts_hbm, res_hbm, out_ref, tab_ref, ids_ref, pts_ref, res_ref, sems, *, n_plane, n_col):
    me = info[2]
    rows = pts_ref.shape[0]
    ids_in = pltpu.make_async_copy(ids_hbm, ids_ref, sems.at[0])
    pts_in = pltpu.make_async_copy(pts_hbm, pts_ref, sems.at[1])
    res_in = pltpu.make_async_copy(res_hbm, res_ref, sems.at[2])
    ids_in.start()
    pts_in.start()
    res_in.start()
    ids_in.wait()
    ids = ids_ref[...]
    n = ids.shape[1]
    eye = iota((n, n), 0) == iota((n, n), 1)
    ids_col = jnp.sum(jnp.where(eye, jnp.broadcast_to(ids, (n, n)), 0), axis=1, keepdims=True)
    owner = ids // rows
    column = ids // (rows * n_col)
    less = jnp.broadcast_to(ids_col, (n, n)) < ids
    rank = jnp.sum(jnp.where(less & (ids_col >= column * (rows * n_col)), 1, 0), axis=0, keepdims=True)
    slot = jnp.sum(jnp.where(less & (ids_col >= owner * rows), 1, 0), axis=0, keepdims=True)
    planes = COL_CAP * n_plane
    straight = column * COL_CAP + rank
    turned = planes - COL_CAP - column * COL_CAP + rank
    here = jnp.where(info[0] == 0, straight, turned)
    there = jnp.where(info[0] == 0, turned, straight)
    tab_ref[...] = jnp.concatenate([ids, rank, slot, here, there, jnp.zeros((3, n), I32)], axis=0)
    mine = owner == me
    lane = iota((8, rows), 1)
    sub = iota((8, rows), 0)
    take = jnp.zeros((8, rows), F32)
    for k in range(CAP):
        at = jnp.max(jnp.where(mine & (slot == k), ids - me * rows, -1), axis=1, keepdims=True)
        take = jnp.where((sub == k) & (lane == at), 1.0, take)
    take = take.astype(BF)
    pts_in.wait()
    picked = dot(take, pts_ref[...]).astype(BF)
    res_in.wait()
    res = res_ref[...]
    hi = res.astype(BF)
    low = (res - hi.astype(F32)).astype(BF)
    classes = res.shape[0]
    pad = jnp.zeros((8, CLASS_PAD - classes), F32)
    parts = [jnp.concatenate([dot(take, v, NT), pad], axis=1).astype(BF) for v in (hi, low)]
    half = pts_ref.shape[1] // 2
    chalf = CLASS_PAD // 2
    for core in range(2):
        row = [picked[:CAP, core * half : (core + 1) * half]]
        row += [v[:CAP, core * CLASS_STEP : core * CLASS_STEP + chalf] for v in parts]
        row = jnp.concatenate(row, axis=1).astype(F32)
        w = row.shape[1] // SPLIT
        block = jnp.concatenate([row[:, q * w : (q + 1) * w] for q in range(SPLIT)], axis=0).astype(BF)
        for z in range(n_col // 2):
            out_ref[2 * z + core] = block


def pack(info, ids, points, res_t, n_plane, n_col):
    width = points.shape[1] // 2 + CLASS_PAD
    n = ids.shape[1]
    return pl.pallas_call(
        functools.partial(pack_body, n_plane=n_plane, n_col=n_col),
        out_shape=(
            jax.ShapeDtypeStruct((n_col, CAP * SPLIT, width // SPLIT), BF),
            jax.ShapeDtypeStruct((8, n), I32),
        ),
        in_specs=[smem(), hbm(), hbm(), hbm()],
        out_specs=(vmem(), vmem()),
        scratch_shapes=[
            pltpu.VMEM(ids.shape, I32),
            pltpu.VMEM(points.shape, BF),
            pltpu.VMEM(res_t.shape, F32),
            pltpu.SemaphoreType.DMA((3,)),
        ],
        compiler_params=params(60),
    )(info, ids, points, res_t)


def table(tab_ref):
    return tab_ref[0:1, :], tab_ref[1:2, :], tab_ref[2:3, :]


def encode(res):
    top = jnp.max(jnp.abs(res), axis=1, keepdims=True)
    power = jnp.floor(jnp.log2(jnp.maximum(top, 1e-30))) + 1.0
    code = jnp.floor(res * (FRACTION / jnp.exp2(power)) + 0.5).astype(I32)
    code = jnp.where(iota(res.shape, 1) == SCALE_LANE, power.astype(I32) * 16, code)
    low = code & 15
    part = res.shape[1] // 4
    word = low[:, :part]
    for k in range(1, 4):
        word = word | (low[:, k * part : (k + 1) * part] << (4 * k))
    return jnp.concatenate([code >> 4, word - 32768], axis=1).astype(jnp.int16)


def decode(words):
    words = words.astype(I32)
    n = words.shape[1] * 4 // 5
    high = words[:, :n]
    word = words[:, n:] + 32768
    low = jnp.concatenate([(word >> (4 * k)) & 15 for k in range(4)], axis=1)
    unit = jnp.exp2(high[:, SCALE_LANE : SCALE_LANE + 1].astype(F32)) * (1.0 / FRACTION)
    return (high * 16 + low).astype(F32) * unit


def compact_body(info, tab_ref, in_ref, pts_ref, res_ref, *, rows, n_col):
    plane = info[1]
    ids, rank, slot = table(tab_ref)
    n = ids.shape[1]
    owner = ids // rows
    column = ids // (rows * n_col)
    wide = in_ref.shape[0]
    sel_rank = (iota((COL_CAP, n), 0) == rank) & (column == plane)
    at = iota((wide, n), 0)
    group = CAP * SPLIT
    sel_slot = (at // group == owner - column * n_col) & (at % CAP == slot)
    pick = dot(sel_rank.astype(F32).astype(BF), sel_slot.astype(F32).astype(BF), NT)
    part = (iota((COL_CAP, wide), 1) // CAP) % SPLIT
    data = in_ref[...]
    whole = [dot(jnp.where(part == q, pick, 0.0).astype(BF), data) for q in range(SPLIT)]
    whole = jnp.concatenate(whole, axis=1)
    half = pts_ref.shape[2]
    pts = whole[:, :half].astype(BF)
    chalf = CLASS_PAD // 2
    res = encode(whole[:, half : half + chalf] + whole[:, half + chalf :])
    for p in range(pts_ref.shape[0]):
        pts_ref[p] = pts
        res_ref[p] = res


def compact(info, tab, data, rows, half, n_plane, n_col):
    return pl.pallas_call(
        functools.partial(compact_body, rows=rows, n_col=n_col),
        out_shape=(
            jax.ShapeDtypeStruct((n_plane, COL_CAP, half), BF),
            jax.ShapeDtypeStruct((n_plane, COL_CAP, CODED), jnp.int16),
        ),
        in_specs=[smem(), vmem(), vmem()],
        out_specs=(vmem(), vmem()),
        compiler_params=params(16),
    )(info, tab, data)


def place_matrix(tab_ref, wide, row=3):
    at = tab_ref[row : row + 1, :]
    return (iota((wide, at.shape[1]), 0) == at).astype(F32).astype(BF)


def order_body(tab_ref, in_ref, out_ref):
    out_ref[...] = dot(place_matrix(tab_ref, in_ref.shape[0]), in_ref[...], TN).astype(BF)


def order(tab, data):
    return pl.pallas_call(
        order_body,
        out_shape=jax.ShapeDtypeStruct((tab.shape[1], data.shape[1]), BF),
        in_specs=[vmem(), vmem()],
        out_specs=vmem(),
        compiler_params=params(10),
    )(tab, data)


def first_half_body(info, pts_ref, own_ref, cross_ref, p_cross_ref, psq_ref, p_oth_ref, *, half):
    core = info[0]
    own = own_ref[...]
    cross_ref[...] = dot(own, own, NT)
    p_own = pts_ref[:, pl.ds(pl.multiple_of(core * half, half), half)]
    p_oth = pts_ref[:, pl.ds(pl.multiple_of((1 - core) * half, half), half)]
    p_cross_ref[...] = dot(p_own, own, NT)
    p_oth_ref[...] = p_oth
    a = p_own.astype(F32)
    b = p_oth.astype(F32)
    psq_ref[...] = jnp.sum(a * a, axis=1, keepdims=True) + jnp.sum(b * b, axis=1, keepdims=True)


def first_half(info, points, own):
    n, half = own.shape
    rows = points.shape[0]
    return pl.pallas_call(
        functools.partial(first_half_body, half=half),
        out_shape=(
            jax.ShapeDtypeStruct((n, n), F32),
            jax.ShapeDtypeStruct((rows, n), F32),
            jax.ShapeDtypeStruct((rows, 1), F32),
            jax.ShapeDtypeStruct((rows, half), BF),
        ),
        in_specs=[smem(), vmem(), vmem()],
        out_specs=(vmem(),) * 4,
        compiler_params=params(12),
        cost_estimate=pl.CostEstimate(flops=10**6, bytes_accessed=10**6, transcendentals=0),
    )(info, points, own)


def inverse_body(info, tab_ref, p_oth_ref, oth_ref, cross_ref, p_cross_ref, psq_ref, hi_ref, lo_ref, g_ref, m_ref, gh_ref, gl_ref, x_ref, *, share):
    n = oth_ref.shape[0]
    rows = p_cross_ref.shape[0]
    me, share_at = info[2], info[3]
    oth = oth_ref[...]
    cross = cross_ref[...] + dot(oth, oth, NT)
    eye = iota((n, n), 0) == iota((n, n), 1)
    diag = jnp.where(eye, cross, 0.0)
    sq_row = jnp.sum(diag, axis=0, keepdims=True)
    sq_col = jnp.sum(diag, axis=1, keepdims=True)
    gram = jnp.exp(-GAMMA * (sq_col + sq_row - 2.0 * cross)) + jnp.where(eye, RIDGE, 0.0)
    g_ref[...] = gram
    gh, gl = two_parts(gram)
    gh_ref[...] = gh
    gl_ref[...] = gl
    p_cross = p_cross_ref[...] + dot(p_oth_ref[...], oth, NT)
    p_kern = jnp.exp(-GAMMA * (psq_ref[...] + sq_row - 2.0 * p_cross))
    point_id = me * rows + iota((rows, n), 0)
    m_ref[pl.ds(0, rows), :] = p_kern + jnp.where(point_id == table(tab_ref)[0], RIDGE, 0.0)
    m_ref[pl.ds(rows, share), :] = jnp.where(share_at + iota((share, n), 0) == iota((share, n), 1), 1.0, 0.0)
    lo = 0.499
    gram = g_ref[...]
    v_col = jnp.sum(gram, axis=1, keepdims=True)
    v_row = jnp.sum(gram, axis=0, keepdims=True)
    hi = jnp.max(jnp.sum(gram * v_col, axis=0, keepdims=True) / v_row) * 1.001
    s = 2.0 / (lo + hi)
    x_ref[...] = jnp.where(eye, 2.0 * s, 0.0) - (s * s) * gram
    d = (hi - lo) / (hi + lo)

    def refine(resid, whole):
        x = x_ref[...] * (2.0 / (2.0 - resid))
        xh, xl = two_parts(x)
        gh = gh_ref[...]
        gx = dot(gh, xh) + (dot(gh, xl) + dot(gl_ref[...], xh) if whole else dot(gh, xl))
        r = (jnp.where(eye, 1.0, 0.0) - gx).astype(BF)
        x_ref[...] = x + (dot(xh, r) + dot(xl, r))
        after = resid / (2.0 - resid)
        return after * after

    resid = lax.while_loop(lambda v: v > 0.5, functools.partial(refine, whole=False), d * d)
    lax.while_loop(lambda v: v > 0.02, functools.partial(refine, whole=True), resid)
    xh, xl = two_parts(x_ref[...])
    m = m_ref[...]
    w = mm3(two_parts(m), (xh, xl))
    e = (m - mm3(two_parts(w), (gh_ref[...], gl_ref[...]))).astype(BF)
    w = w + (dot(e, xh) + dot(e, xl))
    e = (m - dot(w, g_ref[...], NN, HI)).astype(BF)
    w = w + (dot(e, xh) + dot(e, xl))
    wh, wl = two_parts(w)
    hi_ref[...] = wh
    lo_ref[...] = wl


def inverse(info, tab, p_oth, oth, cross, p_cross, psq, share):
    n = oth.shape[0]
    rows = p_oth.shape[0]
    out = jax.ShapeDtypeStruct((rows + share, n), BF)
    return pl.pallas_call(
        functools.partial(inverse_body, share=share),
        out_shape=(out, out),
        in_specs=[smem()] + [vmem()] * 6,
        out_specs=(vmem(), vmem()),
        scratch_shapes=[
            pltpu.VMEM((n, n), F32),
            pltpu.VMEM((rows + share, n), F32),
            pltpu.VMEM((n, n), BF),
            pltpu.VMEM((n, n), BF),
            pltpu.VMEM((n, n), F32),
        ],
        compiler_params=params(18),
        cost_estimate=pl.CostEstimate(flops=12 * 10**9, bytes_accessed=6 * 10**6, transcendentals=4 * 10**5),
    )(info, tab, p_oth, oth, cross, p_cross, psq)


def apply_weights(hi, lo, res_ref):
    return mm3((hi, lo), two_parts(decode(res_ref[...])))


def update_own_body(tab_ref, wh_ref, wl_ref, res_ref, hi_ref, lo_ref, ch_ref):
    wide = res_ref.shape[0]
    here = place_matrix(tab_ref, wide)
    hi = dot(wh_ref[...], here, NT).astype(BF)
    lo = dot(wl_ref[...], here, NT).astype(BF)
    ch_ref[...] = apply_weights(hi, lo, res_ref)
    there = place_matrix(tab_ref, wide, 4)
    hi_ref[...] = dot(wh_ref[...], there, NT).astype(BF)
    lo_ref[...] = dot(wl_ref[...], there, NT).astype(BF)


def update_own(tab, wh, wl, res):
    m = wh.shape[0]
    wide = res.shape[0]
    out = jax.ShapeDtypeStruct((m, wide), BF)
    return pl.pallas_call(
        update_own_body,
        out_shape=(out, out, jax.ShapeDtypeStruct((m, CLASS_PAD // 2), F32)),
        in_specs=[vmem()] * 4,
        out_specs=(vmem(),) * 3,
        compiler_params=params(10),
        cost_estimate=pl.CostEstimate(flops=2 * 10**9, bytes_accessed=4 * 10**6, transcendentals=0),
    )(tab, wh, wl, res)


def update_other_body(info, hi_ref, lo_ref, res_ref, ch_ref, res_t_ref, out_ref, share_ref):
    core = info[0]
    classes, rows = res_t_ref.shape
    skip = 2 * CLASS_SPAN - classes
    mine = ch_ref[...]
    theirs = apply_weights(hi_ref[...], lo_ref[...], res_ref)
    low = jnp.where(core == 0, mine, theirs)
    high = jnp.where(core == 0, theirs, mine)
    share_ref[...] = jnp.concatenate([low[rows:, :CLASS_SPAN], high[rows:, skip:CLASS_SPAN]], axis=1)
    out_ref[:CLASS_SPAN, :] = res_t_ref[:CLASS_SPAN, :] - low[:rows].T[:CLASS_SPAN]
    out_ref[CLASS_SPAN:, :] = res_t_ref[CLASS_SPAN:, :] - high[:rows].T[skip:CLASS_SPAN]


def update_other(info, hi, lo, res, change, res_t, share):
    classes, rows = res_t.shape
    return pl.pallas_call(
        update_other_body,
        out_shape=(jax.ShapeDtypeStruct((classes, rows), F32), jax.ShapeDtypeStruct((share, classes), F32)),
        in_specs=[smem()] + [vmem()] * 5,
        out_specs=(vmem(), vmem()),
        compiler_params=params(16),
    )(info, hi, lo, res, change, res_t)


def plane_groups():
    groups = []
    for place in range(32):
        members = [p * 32 + place for p in range(16)]
        groups.append(members if place % 2 == 0 else members[::-1])
    return groups


def over_plane(value):
    return lax.all_to_all(value, EVERY, 0, 0, axis_index_groups=plane_groups(), tiled=True)


def on_device(points, residual, block_ids):
    rows, feats = points.shape
    block = block_ids.shape[0]
    n_plane = lax.axis_size(PLANE)
    n_col = lax.axis_size(COLUMN)
    n_gy = lax.axis_size("zl") * lax.axis_size("c")
    plane = lax.axis_index(PLANE)
    place = lax.axis_index(COLUMN)
    share = block // n_gy
    half = feats // 2
    wide = n_plane * COL_CAP
    info = jnp.stack([lax.axis_index("c"), plane, plane * n_col + place, (place % n_gy) * share]).astype(I32)
    ids = block_ids.reshape(1, block)
    res_t = residual.T
    swap = [(0, 1), (1, 0)]

    packed, tab = pack(info, ids, points, res_t, n_plane, n_col)
    col_rows = lax.all_to_all(packed, COLUMN, 0, 0, tiled=True)
    col_rows = col_rows.reshape(n_col * CAP * SPLIT, col_rows.shape[2])
    pts_out, res_out = compact(info, tab, col_rows, rows, half, n_plane, n_col)
    all_pts = over_plane(pts_out).reshape(wide, half)
    all_res = over_plane(res_out).reshape(wide, CODED)
    own = order(tab, all_pts)
    other = lax.ppermute(own, "c", swap)
    cross, p_cross, psq, p_oth = first_half(info, points, own)
    wh, wl = inverse(info, tab, p_oth, other, cross, p_cross, psq, share)
    all_res, wh = lax.optimization_barrier((all_res, wh))
    other_res = lax.ppermute(all_res, "c", swap)
    hi, lo, change = update_own(tab, wh, wl, all_res)
    out_t, step_share = update_other(info, hi, lo, other_res, change, res_t, share)
    return (out_t.T, step_share)


def solution(mesh):
    fine = Mesh(mesh.devices.reshape(4, 4, 2, 8, 2), EVERY)
    return jax.shard_map(
        on_device,
        mesh=fine,
        in_specs=(P(EVERY, None), P(EVERY, None), P()),
        out_specs=(P(EVERY, None), P(("zl", "c"), None)),
        check_vma=False,
    )
```

```python
import functools

import jax
import jax.numpy as jnp
from jax import lax
from jax.experimental import pallas as pl
from jax.experimental.pallas import tpu as pltpu
from jax.sharding import Mesh
from jax.sharding import PartitionSpec as P

F32 = jnp.float32
BF = jnp.bfloat16
I32 = jnp.int32
HI = lax.Precision.HIGHEST
NN = (((1,), (0,)), ((), ()))
NT = (((1,), (1,)), ((), ()))
TN = (((0,), (0,)), ((), ()))

GAMMA = 0.125
RIDGE = 0.5
PLANE = ("y", "x")
COLUMN = ("zh", "zl", "c")
EVERY = PLANE + COLUMN
CAP = 2
COL_CAP = 48
CLASS_PAD = 1024
SPLIT = 4
CLASS_STEP = 496
CLASS_SPAN = 504
SCALE_LANE = 511
FRACTION = 2.0**22
MIB = 1024 * 1024


def dot(a, b, dn=NN, prec=None):
    return lax.dot_general(a, b, dn, preferred_element_type=F32, precision=prec)


def iota(shape, axis):
    return lax.broadcasted_iota(I32, shape, axis)


def two_parts(v):
    hi = v.astype(BF)
    return hi, (v - hi.astype(F32)).astype(BF)


def mm3(a, b):
    ah, al = a
    bh, bl = b
    return dot(ah, bh) + (dot(ah, bl) + dot(al, bh))


def vmem():
    return pl.BlockSpec(memory_space=pltpu.VMEM)


def hbm():
    return pl.BlockSpec(memory_space=pltpu.HBM)


def params(mib):
    return pltpu.CompilerParams(vmem_limit_bytes=mib * MIB)


def my_core():
    return lax.axis_index("c")


def my_plane():
    return lax.axis_index("y") * 4 + lax.axis_index("x")


def my_place():
    return (lax.axis_index("zh") * 8 + lax.axis_index("zl")) * 2 + my_core()


def pack_body(ids_hbm, pts_hbm, res_hbm, out_ref, tab_ref, ids_ref, pts_ref, res_ref, sems, *, n_plane, n_col):
    me = my_plane() * n_col + my_place()
    rows = pts_ref.shape[0]
    ids_in = pltpu.make_async_copy(ids_hbm, ids_ref, sems.at[0])
    pts_in = pltpu.make_async_copy(pts_hbm, pts_ref, sems.at[1])
    res_in = pltpu.make_async_copy(res_hbm, res_ref, sems.at[2])
    ids_in.start()
    pts_in.start()
    res_in.start()
    ids_in.wait()
    ids = ids_ref[...]
    n = ids.shape[1]
    eye = iota((n, n), 0) == iota((n, n), 1)
    ids_col = jnp.sum(jnp.where(eye, jnp.broadcast_to(ids, (n, n)), 0), axis=1, keepdims=True)
    owner = ids // rows
    column = ids // (rows * n_col)
    less = jnp.broadcast_to(ids_col, (n, n)) < ids
    rank = jnp.sum(jnp.where(less & (ids_col >= column * (rows * n_col)), 1, 0), axis=0, keepdims=True)
    slot = jnp.sum(jnp.where(less & (ids_col >= owner * rows), 1, 0), axis=0, keepdims=True)
    planes = COL_CAP * n_plane
    straight = column * COL_CAP + rank
    turned = planes - COL_CAP - column * COL_CAP + rank
    here = jnp.where(my_core() == 0, straight, turned)
    there = jnp.where(my_core() == 0, turned, straight)
    tab_ref[...] = jnp.concatenate([ids, rank, slot, here, there, jnp.zeros((3, n), I32)], axis=0)
    mine = owner == me
    lane = iota((8, rows), 1)
    sub = iota((8, rows), 0)
    take = jnp.zeros((8, rows), F32)
    for k in range(CAP):
        at = jnp.max(jnp.where(mine & (slot == k), ids - me * rows, -1), axis=1, keepdims=True)
        take = jnp.where((sub == k) & (lane == at), 1.0, take)
    take = take.astype(BF)
    pts_in.wait()
    picked = dot(take, pts_ref[...]).astype(BF)
    res_in.wait()
    res = res_ref[...]
    hi = res.astype(BF)
    low = (res - hi.astype(F32)).astype(BF)
    classes = res.shape[0]
    pad = jnp.zeros((8, CLASS_PAD - classes), F32)
    parts = [jnp.concatenate([dot(take, v, NT), pad], axis=1).astype(BF) for v in (hi, low)]
    half = pts_ref.shape[1] // 2
    chalf = CLASS_PAD // 2
    for core in range(2):
        row = [picked[:CAP, core * half : (core + 1) * half]]
        row += [v[:CAP, core * CLASS_STEP : core * CLASS_STEP + chalf] for v in parts]
        row = jnp.concatenate(row, axis=1).astype(F32)
        w = row.shape[1] // SPLIT
        block = jnp.concatenate([row[:, q * w : (q + 1) * w] for q in range(SPLIT)], axis=0).astype(BF)
        for z in range(n_col // 2):
            out_ref[2 * z + core] = block


def pack(ids, points, res_t, n_plane, n_col):
    width = points.shape[1] // 2 + CLASS_PAD
    n = ids.shape[1]
    return pl.pallas_call(
        functools.partial(pack_body, n_plane=n_plane, n_col=n_col),
        out_shape=(
            jax.ShapeDtypeStruct((n_col, CAP * SPLIT, width // SPLIT), BF),
            jax.ShapeDtypeStruct((8, n), I32),
        ),
        in_specs=[hbm(), hbm(), hbm()],
        out_specs=(vmem(), vmem()),
        scratch_shapes=[
            pltpu.VMEM(ids.shape, I32),
            pltpu.VMEM(points.shape, BF),
            pltpu.VMEM(res_t.shape, F32),
            pltpu.SemaphoreType.DMA((3,)),
        ],
        compiler_params=params(60),
    )(ids, points, res_t)


def table(tab_ref):
    return tab_ref[0:1, :], tab_ref[1:2, :], tab_ref[2:3, :]


def encode(res):
    top = jnp.max(jnp.abs(res), axis=1, keepdims=True)
    power = jnp.floor(jnp.log2(jnp.maximum(top, 1e-30))) + 1.0
    code = jnp.floor(res * (FRACTION / jnp.exp2(power)) + 0.5).astype(I32)
    code = jnp.where(iota(res.shape, 1) == SCALE_LANE, power.astype(I32) * 256, code)
    low = code & 255
    half = res.shape[1] // 2
    pair = (low[:, :half] | (low[:, half:] << 8)) - 32768
    return jnp.concatenate([code >> 8, pair], axis=1).astype(jnp.int16)


def decode(words):
    words = words.astype(I32)
    n = words.shape[1] * 2 // 3
    high = words[:, :n]
    pair = words[:, n:] + 32768
    low = jnp.concatenate([pair & 255, pair >> 8], axis=1)
    unit = jnp.exp2(high[:, SCALE_LANE : SCALE_LANE + 1].astype(F32)) * (1.0 / FRACTION)
    return (high * 256 + low).astype(F32) * unit


def compact_body(tab_ref, in_ref, pts_ref, res_ref, *, rows, n_col):
    plane = my_plane()
    ids, rank, slot = table(tab_ref)
    n = ids.shape[1]
    owner = ids // rows
    column = ids // (rows * n_col)
    wide = in_ref.shape[0]
    sel_rank = (iota((COL_CAP, n), 0) == rank) & (column == plane)
    at = iota((wide, n), 0)
    group = CAP * SPLIT
    sel_slot = (at // group == owner - column * n_col) & (at % CAP == slot)
    pick = dot(sel_rank.astype(F32).astype(BF), sel_slot.astype(F32).astype(BF), NT)
    part = (iota((COL_CAP, wide), 1) // CAP) % SPLIT
    data = in_ref[...]
    whole = [dot(jnp.where(part == q, pick, 0.0).astype(BF), data) for q in range(SPLIT)]
    whole = jnp.concatenate(whole, axis=1)
    half = pts_ref.shape[2]
    pts = whole[:, :half].astype(BF)
    chalf = CLASS_PAD // 2
    res = encode(whole[:, half : half + chalf] + whole[:, half + chalf :])
    for p in range(pts_ref.shape[0]):
        pts_ref[p] = pts
        res_ref[p] = res


def compact(tab, data, rows, half, n_plane, n_col):
    return pl.pallas_call(
        functools.partial(compact_body, rows=rows, n_col=n_col),
        out_shape=(
            jax.ShapeDtypeStruct((n_plane, COL_CAP, half), BF),
            jax.ShapeDtypeStruct((n_plane, COL_CAP, CLASS_PAD * 3 // 4), jnp.int16),
        ),
        in_specs=[vmem(), vmem()],
        out_specs=(vmem(), vmem()),
        compiler_params=params(16),
    )(tab, data)


def place_matrix(tab_ref, wide, row=3):
    at = tab_ref[row : row + 1, :]
    return (iota((wide, at.shape[1]), 0) == at).astype(F32).astype(BF)


def order_body(tab_ref, in_ref, out_ref):
    out_ref[...] = dot(place_matrix(tab_ref, in_ref.shape[0]), in_ref[...], TN).astype(BF)


def order(tab, data):
    return pl.pallas_call(
        order_body,
        out_shape=jax.ShapeDtypeStruct((tab.shape[1], data.shape[1]), BF),
        in_specs=[vmem(), vmem()],
        out_specs=vmem(),
        compiler_params=params(10),
    )(tab, data)


def first_half_body(pts_ref, own_ref, cross_ref, p_cross_ref, psq_ref, p_oth_ref, *, half):
    core = my_core()
    own = own_ref[...]
    cross_ref[...] = dot(own, own, NT)
    p_own = pts_ref[:, pl.ds(pl.multiple_of(core * half, half), half)]
    p_oth = pts_ref[:, pl.ds(pl.multiple_of((1 - core) * half, half), half)]
    p_cross_ref[...] = dot(p_own, own, NT)
    p_oth_ref[...] = p_oth
    a = p_own.astype(F32)
    b = p_oth.astype(F32)
    psq_ref[...] = jnp.sum(a * a, axis=1, keepdims=True) + jnp.sum(b * b, axis=1, keepdims=True)


def first_half(points, own):
    n, half = own.shape
    rows = points.shape[0]
    return pl.pallas_call(
        functools.partial(first_half_body, half=half),
        out_shape=(
            jax.ShapeDtypeStruct((n, n), F32),
            jax.ShapeDtypeStruct((rows, n), F32),
            jax.ShapeDtypeStruct((rows, 1), F32),
            jax.ShapeDtypeStruct((rows, half), BF),
        ),
        in_specs=[vmem(), vmem()],
        out_specs=(vmem(),) * 4,
        compiler_params=params(12),
        cost_estimate=pl.CostEstimate(flops=10**6, bytes_accessed=10**6, transcendentals=0),
    )(points, own)


def inverse_body(tab_ref, p_oth_ref, oth_ref, cross_ref, p_cross_ref, psq_ref, hi_ref, lo_ref, g_ref, m_ref, gh_ref, gl_ref, x_ref, *, share):
    n = oth_ref.shape[0]
    rows = p_cross_ref.shape[0]
    me = my_plane() * 32 + my_place()
    share_at = lax.rem(my_place(), 16) * share
    oth = oth_ref[...]
    cross = cross_ref[...] + dot(oth, oth, NT)
    eye = iota((n, n), 0) == iota((n, n), 1)
    diag = jnp.where(eye, cross, 0.0)
    sq_row = jnp.sum(diag, axis=0, keepdims=True)
    sq_col = jnp.sum(diag, axis=1, keepdims=True)
    gram = jnp.exp(-GAMMA * (sq_col + sq_row - 2.0 * cross)) + jnp.where(eye, RIDGE, 0.0)
    g_ref[...] = gram
    gh, gl = two_parts(gram)
    gh_ref[...] = gh
    gl_ref[...] = gl
    p_cross = p_cross_ref[...] + dot(p_oth_ref[...], oth, NT)
    p_kern = jnp.exp(-GAMMA * (psq_ref[...] + sq_row - 2.0 * p_cross))
    point_id = me * rows + iota((rows, n), 0)
    m_ref[pl.ds(0, rows), :] = p_kern + jnp.where(point_id == table(tab_ref)[0], RIDGE, 0.0)
    m_ref[pl.ds(rows, share), :] = jnp.where(share_at + iota((share, n), 0) == iota((share, n), 1), 1.0, 0.0)
    lo = 0.499
    gram = g_ref[...]
    v_col = jnp.sum(gram, axis=1, keepdims=True)
    v_row = jnp.sum(gram, axis=0, keepdims=True)
    hi = jnp.max(jnp.sum(gram * v_col, axis=0, keepdims=True) / v_row) * 1.001
    s = 2.0 / (lo + hi)
    x_ref[...] = jnp.where(eye, 2.0 * s, 0.0) - (s * s) * gram
    d = (hi - lo) / (hi + lo)

    def refine(resid, whole):
        x = x_ref[...] * (2.0 / (2.0 - resid))
        xh, xl = two_parts(x)
        gh = gh_ref[...]
        gx = dot(gh, xh) + (dot(gh, xl) + dot(gl_ref[...], xh) if whole else dot(gh, xl))
        r = (jnp.where(eye, 1.0, 0.0) - gx).astype(BF)
        x_ref[...] = x + (dot(xh, r) + dot(xl, r))
        after = resid / (2.0 - resid)
        return after * after

    resid = lax.while_loop(lambda v: v > 0.5, functools.partial(refine, whole=False), d * d)
    lax.while_loop(lambda v: v > 0.02, functools.partial(refine, whole=True), resid)
    xh, xl = two_parts(x_ref[...])
    m = m_ref[...]
    w = mm3(two_parts(m), (xh, xl))
    e = (m - mm3(two_parts(w), (gh_ref[...], gl_ref[...]))).astype(BF)
    w = w + (dot(e, xh) + dot(e, xl))
    e = (m - dot(w, g_ref[...], NN, HI)).astype(BF)
    w = w + (dot(e, xh) + dot(e, xl))
    wh, wl = two_parts(w)
    hi_ref[...] = wh
    lo_ref[...] = wl


def inverse(tab, p_oth, oth, cross, p_cross, psq, share):
    n = oth.shape[0]
    rows = p_oth.shape[0]
    out = jax.ShapeDtypeStruct((rows + share, n), BF)
    return pl.pallas_call(
        functools.partial(inverse_body, share=share),
        out_shape=(out, out),
        in_specs=[vmem()] * 6,
        out_specs=(vmem(), vmem()),
        scratch_shapes=[
            pltpu.VMEM((n, n), F32),
            pltpu.VMEM((rows + share, n), F32),
            pltpu.VMEM((n, n), BF),
            pltpu.VMEM((n, n), BF),
            pltpu.VMEM((n, n), F32),
        ],
        compiler_params=params(18),
        cost_estimate=pl.CostEstimate(flops=10**6, bytes_accessed=10**6, transcendentals=0),
    )(tab, p_oth, oth, cross, p_cross, psq)


def apply_weights(hi, lo, res_ref):
    return mm3((hi, lo), two_parts(decode(res_ref[...])))


def update_own_body(tab_ref, wh_ref, wl_ref, res_ref, hi_ref, lo_ref, ch_ref):
    wide = res_ref.shape[0]
    here = place_matrix(tab_ref, wide)
    hi = dot(wh_ref[...], here, NT).astype(BF)
    lo = dot(wl_ref[...], here, NT).astype(BF)
    ch_ref[...] = apply_weights(hi, lo, res_ref)
    there = place_matrix(tab_ref, wide, 4)
    hi_ref[...] = dot(wh_ref[...], there, NT).astype(BF)
    lo_ref[...] = dot(wl_ref[...], there, NT).astype(BF)


def update_own(tab, wh, wl, res):
    m = wh.shape[0]
    wide = res.shape[0]
    out = jax.ShapeDtypeStruct((m, wide), BF)
    return pl.pallas_call(
        update_own_body,
        out_shape=(out, out, jax.ShapeDtypeStruct((m, CLASS_PAD // 2), F32)),
        in_specs=[vmem()] * 4,
        out_specs=(vmem(),) * 3,
        compiler_params=params(10),
        cost_estimate=pl.CostEstimate(flops=2 * 10**9, bytes_accessed=4 * 10**6, transcendentals=0),
    )(tab, wh, wl, res)


def update_other_body(hi_ref, lo_ref, res_ref, ch_ref, res_t_ref, out_ref, share_ref):
    core = my_core()
    classes, rows = res_t_ref.shape
    skip = 2 * CLASS_SPAN - classes
    mine = ch_ref[...]
    theirs = apply_weights(hi_ref[...], lo_ref[...], res_ref)
    low = jnp.where(core == 0, mine, theirs)
    high = jnp.where(core == 0, theirs, mine)
    share_ref[...] = jnp.concatenate([low[rows:, :CLASS_SPAN], high[rows:, skip:CLASS_SPAN]], axis=1)
    out_ref[:CLASS_SPAN, :] = res_t_ref[:CLASS_SPAN, :] - low[:rows].T[:CLASS_SPAN]
    out_ref[CLASS_SPAN:, :] = res_t_ref[CLASS_SPAN:, :] - high[:rows].T[skip:CLASS_SPAN]


def update_other(hi, lo, res, change, res_t, share):
    classes, rows = res_t.shape
    return pl.pallas_call(
        update_other_body,
        out_shape=(jax.ShapeDtypeStruct((classes, rows), F32), jax.ShapeDtypeStruct((share, classes), F32)),
        in_specs=[vmem()] * 5,
        out_specs=(vmem(), vmem()),
        compiler_params=params(16),
    )(hi, lo, res, change, res_t)


def plane_groups():
    groups = []
    for place in range(32):
        members = [p * 32 + place for p in range(16)]
        groups.append(members if place % 2 == 0 else members[::-1])
    return groups


def over_plane(value):
    return lax.all_to_all(value, EVERY, 0, 0, axis_index_groups=plane_groups(), tiled=True)


def on_device(points, residual, block_ids):
    rows, feats = points.shape
    block = block_ids.shape[0]
    n_plane = lax.axis_size(PLANE)
    n_col = lax.axis_size(COLUMN)
    n_gy = lax.axis_size("zl") * lax.axis_size("c")
    plane = lax.axis_index(PLANE)
    place = lax.axis_index(COLUMN)
    share = block // n_gy
    half = feats // 2
    wide = n_plane * COL_CAP
    ids = block_ids.reshape(1, block)
    res_t = residual.T
    swap = [(0, 1), (1, 0)]

    packed, tab = pack(ids, points, res_t, n_plane, n_col)
    col_rows = lax.all_to_all(packed, COLUMN, 0, 0, tiled=True)
    col_rows = col_rows.reshape(n_col * CAP * SPLIT, col_rows.shape[2])
    pts_out, res_out = compact(tab, col_rows, rows, half, n_plane, n_col)
    all_pts = over_plane(pts_out).reshape(wide, half)
    all_res = over_plane(res_out).reshape(wide, CLASS_PAD * 3 // 4)
    own = order(tab, all_pts)
    other = lax.ppermute(own, "c", swap)
    cross, p_cross, psq, p_oth = first_half(points, own)
    wh, wl = inverse(tab, p_oth, other, cross, p_cross, psq, share)
    all_res, wh = lax.optimization_barrier((all_res, wh))
    other_res = lax.ppermute(all_res, "c", swap)
    hi, lo, change = update_own(tab, wh, wl, all_res)
    out_t, step_share = update_other(hi, lo, other_res, change, res_t, share)
    return (out_t.T, step_share)


def solution(mesh):
    fine = Mesh(mesh.devices.reshape(4, 4, 2, 8, 2), EVERY)
    return jax.shard_map(
        on_device,
        mesh=fine,
        in_specs=(P(EVERY, None), P(EVERY, None), P()),
        out_specs=(P(EVERY, None), P(("zl", "c"), None)),
        check_vma=False,
    )
```

```python
import functools

import jax
import jax.numpy as jnp
from jax import lax
from jax.experimental import pallas as pl
from jax.experimental.pallas import tpu as pltpu
from jax.sharding import Mesh
from jax.sharding import PartitionSpec as P

F32 = jnp.float32
BF = jnp.bfloat16
I32 = jnp.int32
HI = lax.Precision.HIGHEST
NN = (((1,), (0,)), ((), ()))
NT = (((1,), (1,)), ((), ()))
TN = (((0,), (0,)), ((), ()))

GAMMA = 0.125
RIDGE = 0.5
PLANE = ("y", "x")
COLUMN = ("zh", "zl", "c")
EVERY = PLANE + COLUMN
CAP = 2
COL_CAP = 48
CLASS_PAD = 1024
SPLIT = 4
CLASS_STEP = 496
CLASS_SPAN = 504
SCALE_LANE = 511
FRACTION = 500000.0
CODED = 640
MIB = 1024 * 1024


def dot(a, b, dn=NN, prec=None):
    return lax.dot_general(a, b, dn, preferred_element_type=F32, precision=prec)


def iota(shape, axis):
    return lax.broadcasted_iota(I32, shape, axis)


def two_parts(v):
    hi = v.astype(BF)
    return hi, (v - hi.astype(F32)).astype(BF)


def mm3(a, b):
    ah, al = a
    bh, bl = b
    return dot(ah, bh) + (dot(ah, bl) + dot(al, bh))


def vmem():
    return pl.BlockSpec(memory_space=pltpu.VMEM)


def hbm():
    return pl.BlockSpec(memory_space=pltpu.HBM)


def params(mib):
    return pltpu.CompilerParams(vmem_limit_bytes=mib * MIB)


def my_core():
    return lax.axis_index("c")


def my_plane():
    return lax.axis_index("y") * 4 + lax.axis_index("x")


def my_place():
    return (lax.axis_index("zh") * 8 + lax.axis_index("zl")) * 2 + my_core()


def pack_body(ids_hbm, pts_hbm, res_hbm, out_ref, tab_ref, ids_ref, pts_ref, res_ref, sems, *, n_plane, n_col):
    me = my_plane() * n_col + my_place()
    rows = pts_ref.shape[0]
    ids_in = pltpu.make_async_copy(ids_hbm, ids_ref, sems.at[0])
    pts_in = pltpu.make_async_copy(pts_hbm, pts_ref, sems.at[1])
    res_in = pltpu.make_async_copy(res_hbm, res_ref, sems.at[2])
    ids_in.start()
    pts_in.start()
    res_in.start()
    ids_in.wait()
    ids = ids_ref[...]
    n = ids.shape[1]
    eye = iota((n, n), 0) == iota((n, n), 1)
    ids_col = jnp.sum(jnp.where(eye, jnp.broadcast_to(ids, (n, n)), 0), axis=1, keepdims=True)
    owner = ids // rows
    column = ids // (rows * n_col)
    less = jnp.broadcast_to(ids_col, (n, n)) < ids
    rank = jnp.sum(jnp.where(less & (ids_col >= column * (rows * n_col)), 1, 0), axis=0, keepdims=True)
    slot = jnp.sum(jnp.where(less & (ids_col >= owner * rows), 1, 0), axis=0, keepdims=True)
    planes = COL_CAP * n_plane
    straight = column * COL_CAP + rank
    turned = planes - COL_CAP - column * COL_CAP + rank
    here = jnp.where(my_core() == 0, straight, turned)
    there = jnp.where(my_core() == 0, turned, straight)
    tab_ref[...] = jnp.concatenate([ids, rank, slot, here, there, jnp.zeros((3, n), I32)], axis=0)
    mine = owner == me
    lane = iota((8, rows), 1)
    sub = iota((8, rows), 0)
    take = jnp.zeros((8, rows), F32)
    for k in range(CAP):
        at = jnp.max(jnp.where(mine & (slot == k), ids - me * rows, -1), axis=1, keepdims=True)
        take = jnp.where((sub == k) & (lane == at), 1.0, take)
    take = take.astype(BF)
    pts_in.wait()
    picked = dot(take, pts_ref[...]).astype(BF)
    res_in.wait()
    res = res_ref[...]
    hi = res.astype(BF)
    low = (res - hi.astype(F32)).astype(BF)
    classes = res.shape[0]
    pad = jnp.zeros((8, CLASS_PAD - classes), F32)
    parts = [jnp.concatenate([dot(take, v, NT), pad], axis=1).astype(BF) for v in (hi, low)]
    half = pts_ref.shape[1] // 2
    chalf = CLASS_PAD // 2
    for core in range(2):
        row = [picked[:CAP, core * half : (core + 1) * half]]
        row += [v[:CAP, core * CLASS_STEP : core * CLASS_STEP + chalf] for v in parts]
        row = jnp.concatenate(row, axis=1).astype(F32)
        w = row.shape[1] // SPLIT
        block = jnp.concatenate([row[:, q * w : (q + 1) * w] for q in range(SPLIT)], axis=0).astype(BF)
        for z in range(n_col // 2):
            out_ref[2 * z + core] = block


def pack(ids, points, res_t, n_plane, n_col):
    width = points.shape[1] // 2 + CLASS_PAD
    n = ids.shape[1]
    return pl.pallas_call(
        functools.partial(pack_body, n_plane=n_plane, n_col=n_col),
        out_shape=(
            jax.ShapeDtypeStruct((n_col, CAP * SPLIT, width // SPLIT), BF),
            jax.ShapeDtypeStruct((8, n), I32),
        ),
        in_specs=[hbm(), hbm(), hbm()],
        out_specs=(vmem(), vmem()),
        scratch_shapes=[
            pltpu.VMEM(ids.shape, I32),
            pltpu.VMEM(points.shape, BF),
            pltpu.VMEM(res_t.shape, F32),
            pltpu.SemaphoreType.DMA((3,)),
        ],
        compiler_params=params(60),
    )(ids, points, res_t)


def table(tab_ref):
    return tab_ref[0:1, :], tab_ref[1:2, :], tab_ref[2:3, :]


def encode(res):
    top = jnp.max(jnp.abs(res), axis=1, keepdims=True)
    power = jnp.floor(jnp.log2(jnp.maximum(top, 1e-30))) + 1.0
    code = jnp.floor(res * (FRACTION / jnp.exp2(power)) + 0.5).astype(I32)
    code = jnp.where(iota(res.shape, 1) == SCALE_LANE, power.astype(I32) * 16, code)
    low = code & 15
    part = res.shape[1] // 4
    word = low[:, :part]
    for k in range(1, 4):
        word = word | (low[:, k * part : (k + 1) * part] << (4 * k))
    return jnp.concatenate([code >> 4, word - 32768], axis=1).astype(jnp.int16)


def decode(words):
    words = words.astype(I32)
    n = words.shape[1] * 4 // 5
    high = words[:, :n]
    word = words[:, n:] + 32768
    low = jnp.concatenate([(word >> (4 * k)) & 15 for k in range(4)], axis=1)
    unit = jnp.exp2(high[:, SCALE_LANE : SCALE_LANE + 1].astype(F32)) * (1.0 / FRACTION)
    return (high * 16 + low).astype(F32) * unit


def compact_body(tab_ref, in_ref, pts_ref, res_ref, *, rows, n_col):
    plane = my_plane()
    ids, rank, slot = table(tab_ref)
    n = ids.shape[1]
    owner = ids // rows
    column = ids // (rows * n_col)
    wide = in_ref.shape[0]
    sel_rank = (iota((COL_CAP, n), 0) == rank) & (column == plane)
    at = iota((wide, n), 0)
    group = CAP * SPLIT
    sel_slot = (at // group == owner - column * n_col) & (at % CAP == slot)
    pick = dot(sel_rank.astype(F32).astype(BF), sel_slot.astype(F32).astype(BF), NT)
    part = (iota((COL_CAP, wide), 1) // CAP) % SPLIT
    data = in_ref[...]
    whole = [dot(jnp.where(part == q, pick, 0.0).astype(BF), data) for q in range(SPLIT)]
    whole = jnp.concatenate(whole, axis=1)
    half = pts_ref.shape[2]
    pts = whole[:, :half].astype(BF)
    chalf = CLASS_PAD // 2
    res = encode(whole[:, half : half + chalf] + whole[:, half + chalf :])
    for p in range(pts_ref.shape[0]):
        pts_ref[p] = pts
        res_ref[p] = res


def compact(tab, data, rows, half, n_plane, n_col):
    return pl.pallas_call(
        functools.partial(compact_body, rows=rows, n_col=n_col),
        out_shape=(
            jax.ShapeDtypeStruct((n_plane, COL_CAP, half), BF),
            jax.ShapeDtypeStruct((n_plane, COL_CAP, CODED), jnp.int16),
        ),
        in_specs=[vmem(), vmem()],
        out_specs=(vmem(), vmem()),
        compiler_params=params(16),
    )(tab, data)


def place_matrix(tab_ref, wide, row=3):
    at = tab_ref[row : row + 1, :]
    return (iota((wide, at.shape[1]), 0) == at).astype(F32).astype(BF)


def order_body(tab_ref, in_ref, out_ref):
    out_ref[...] = dot(place_matrix(tab_ref, in_ref.shape[0]), in_ref[...], TN).astype(BF)


def order(tab, data):
    return pl.pallas_call(
        order_body,
        out_shape=jax.ShapeDtypeStruct((tab.shape[1], data.shape[1]), BF),
        in_specs=[vmem(), vmem()],
        out_specs=vmem(),
        compiler_params=params(10),
    )(tab, data)


def first_half_body(pts_ref, own_ref, cross_ref, p_cross_ref, psq_ref, p_oth_ref, *, half):
    core = my_core()
    own = own_ref[...]
    cross_ref[...] = dot(own, own, NT)
    p_own = pts_ref[:, pl.ds(pl.multiple_of(core * half, half), half)]
    p_oth = pts_ref[:, pl.ds(pl.multiple_of((1 - core) * half, half), half)]
    p_cross_ref[...] = dot(p_own, own, NT)
    p_oth_ref[...] = p_oth
    a = p_own.astype(F32)
    b = p_oth.astype(F32)
    psq_ref[...] = jnp.sum(a * a, axis=1, keepdims=True) + jnp.sum(b * b, axis=1, keepdims=True)


def first_half(points, own):
    n, half = own.shape
    rows = points.shape[0]
    return pl.pallas_call(
        functools.partial(first_half_body, half=half),
        out_shape=(
            jax.ShapeDtypeStruct((n, n), F32),
            jax.ShapeDtypeStruct((rows, n), F32),
            jax.ShapeDtypeStruct((rows, 1), F32),
            jax.ShapeDtypeStruct((rows, half), BF),
        ),
        in_specs=[vmem(), vmem()],
        out_specs=(vmem(),) * 4,
        compiler_params=params(12),
        cost_estimate=pl.CostEstimate(flops=10**6, bytes_accessed=10**6, transcendentals=0),
    )(points, own)


def inverse_body(tab_ref, p_oth_ref, oth_ref, cross_ref, p_cross_ref, psq_ref, hi_ref, lo_ref, g_ref, m_ref, gh_ref, gl_ref, x_ref, *, share):
    n = oth_ref.shape[0]
    rows = p_cross_ref.shape[0]
    me = my_plane() * 32 + my_place()
    share_at = lax.rem(my_place(), 16) * share
    oth = oth_ref[...]
    cross = cross_ref[...] + dot(oth, oth, NT)
    eye = iota((n, n), 0) == iota((n, n), 1)
    diag = jnp.where(eye, cross, 0.0)
    sq_row = jnp.sum(diag, axis=0, keepdims=True)
    sq_col = jnp.sum(diag, axis=1, keepdims=True)
    gram = jnp.exp(-GAMMA * (sq_col + sq_row - 2.0 * cross)) + jnp.where(eye, RIDGE, 0.0)
    g_ref[...] = gram
    gh, gl = two_parts(gram)
    gh_ref[...] = gh
    gl_ref[...] = gl
    p_cross = p_cross_ref[...] + dot(p_oth_ref[...], oth, NT)
    p_kern = jnp.exp(-GAMMA * (psq_ref[...] + sq_row - 2.0 * p_cross))
    point_id = me * rows + iota((rows, n), 0)
    m_ref[pl.ds(0, rows), :] = p_kern + jnp.where(point_id == table(tab_ref)[0], RIDGE, 0.0)
    m_ref[pl.ds(rows, share), :] = jnp.where(share_at + iota((share, n), 0) == iota((share, n), 1), 1.0, 0.0)
    lo = 0.499
    gram = g_ref[...]
    v_col = jnp.sum(gram, axis=1, keepdims=True)
    v_row = jnp.sum(gram, axis=0, keepdims=True)
    hi = jnp.max(jnp.sum(gram * v_col, axis=0, keepdims=True) / v_row) * 1.001
    s = 2.0 / (lo + hi)
    x_ref[...] = jnp.where(eye, 2.0 * s, 0.0) - (s * s) * gram
    d = (hi - lo) / (hi + lo)

    def refine(resid, whole):
        x = x_ref[...] * (2.0 / (2.0 - resid))
        xh, xl = two_parts(x)
        gh = gh_ref[...]
        gx = dot(gh, xh) + (dot(gh, xl) + dot(gl_ref[...], xh) if whole else dot(gh, xl))
        r = (jnp.where(eye, 1.0, 0.0) - gx).astype(BF)
        x_ref[...] = x + (dot(xh, r) + dot(xl, r))
        after = resid / (2.0 - resid)
        return after * after

    resid = lax.while_loop(lambda v: v > 0.5, functools.partial(refine, whole=False), d * d)
    lax.while_loop(lambda v: v > 0.02, functools.partial(refine, whole=True), resid)
    xh, xl = two_parts(x_ref[...])
    m = m_ref[...]
    w = mm3(two_parts(m), (xh, xl))
    e = (m - mm3(two_parts(w), (gh_ref[...], gl_ref[...]))).astype(BF)
    w = w + (dot(e, xh) + dot(e, xl))
    e = (m - dot(w, g_ref[...], NN, HI)).astype(BF)
    w = w + (dot(e, xh) + dot(e, xl))
    wh, wl = two_parts(w)
    hi_ref[...] = wh
    lo_ref[...] = wl


def inverse(tab, p_oth, oth, cross, p_cross, psq, share):
    n = oth.shape[0]
    rows = p_oth.shape[0]
    out = jax.ShapeDtypeStruct((rows + share, n), BF)
    return pl.pallas_call(
        functools.partial(inverse_body, share=share),
        out_shape=(out, out),
        in_specs=[vmem()] * 6,
        out_specs=(vmem(), vmem()),
        scratch_shapes=[
            pltpu.VMEM((n, n), F32),
            pltpu.VMEM((rows + share, n), F32),
            pltpu.VMEM((n, n), BF),
            pltpu.VMEM((n, n), BF),
            pltpu.VMEM((n, n), F32),
        ],
        compiler_params=params(18),
        cost_estimate=pl.CostEstimate(flops=10**6, bytes_accessed=10**6, transcendentals=0),
    )(tab, p_oth, oth, cross, p_cross, psq)


def apply_weights(hi, lo, res_ref):
    return mm3((hi, lo), two_parts(decode(res_ref[...])))


def update_own_body(tab_ref, wh_ref, wl_ref, res_ref, hi_ref, lo_ref, ch_ref):
    wide = res_ref.shape[0]
    here = place_matrix(tab_ref, wide)
    hi = dot(wh_ref[...], here, NT).astype(BF)
    lo = dot(wl_ref[...], here, NT).astype(BF)
    ch_ref[...] = apply_weights(hi, lo, res_ref)
    there = place_matrix(tab_ref, wide, 4)
    hi_ref[...] = dot(wh_ref[...], there, NT).astype(BF)
    lo_ref[...] = dot(wl_ref[...], there, NT).astype(BF)


def update_own(tab, wh, wl, res):
    m = wh.shape[0]
    wide = res.shape[0]
    out = jax.ShapeDtypeStruct((m, wide), BF)
    return pl.pallas_call(
        update_own_body,
        out_shape=(out, out, jax.ShapeDtypeStruct((m, CLASS_PAD // 2), F32)),
        in_specs=[vmem()] * 4,
        out_specs=(vmem(),) * 3,
        compiler_params=params(10),
        cost_estimate=pl.CostEstimate(flops=2 * 10**9, bytes_accessed=4 * 10**6, transcendentals=0),
    )(tab, wh, wl, res)


def update_other_body(hi_ref, lo_ref, res_ref, ch_ref, res_t_ref, out_ref, share_ref):
    core = my_core()
    classes, rows = res_t_ref.shape
    skip = 2 * CLASS_SPAN - classes
    mine = ch_ref[...]
    theirs = apply_weights(hi_ref[...], lo_ref[...], res_ref)
    low = jnp.where(core == 0, mine, theirs)
    high = jnp.where(core == 0, theirs, mine)
    share_ref[...] = jnp.concatenate([low[rows:, :CLASS_SPAN], high[rows:, skip:CLASS_SPAN]], axis=1)
    out_ref[:CLASS_SPAN, :] = res_t_ref[:CLASS_SPAN, :] - low[:rows].T[:CLASS_SPAN]
    out_ref[CLASS_SPAN:, :] = res_t_ref[CLASS_SPAN:, :] - high[:rows].T[skip:CLASS_SPAN]


def update_other(hi, lo, res, change, res_t, share):
    classes, rows = res_t.shape
    return pl.pallas_call(
        update_other_body,
        out_shape=(jax.ShapeDtypeStruct((classes, rows), F32), jax.ShapeDtypeStruct((share, classes), F32)),
        in_specs=[vmem()] * 5,
        out_specs=(vmem(), vmem()),
        compiler_params=params(16),
    )(hi, lo, res, change, res_t)


def plane_groups():
    groups = []
    for place in range(32):
        members = [p * 32 + place for p in range(16)]
        groups.append(members if place % 2 == 0 else members[::-1])
    return groups


def over_plane(value):
    return lax.all_to_all(value, EVERY, 0, 0, axis_index_groups=plane_groups(), tiled=True)


def on_device(points, residual, block_ids):
    rows, feats = points.shape
    block = block_ids.shape[0]
    n_plane = lax.axis_size(PLANE)
    n_col = lax.axis_size(COLUMN)
    n_gy = lax.axis_size("zl") * lax.axis_size("c")
    plane = lax.axis_index(PLANE)
    place = lax.axis_index(COLUMN)
    share = block // n_gy
    half = feats // 2
    wide = n_plane * COL_CAP
    ids = block_ids.reshape(1, block)
    res_t = residual.T
    swap = [(0, 1), (1, 0)]

    packed, tab = pack(ids, points, res_t, n_plane, n_col)
    col_rows = lax.all_to_all(packed, COLUMN, 0, 0, tiled=True)
    col_rows = col_rows.reshape(n_col * CAP * SPLIT, col_rows.shape[2])
    pts_out, res_out = compact(tab, col_rows, rows, half, n_plane, n_col)
    all_pts = over_plane(pts_out).reshape(wide, half)
    all_res = over_plane(res_out).reshape(wide, CODED)
    own = order(tab, all_pts)
    other = lax.ppermute(own, "c", swap)
    cross, p_cross, psq, p_oth = first_half(points, own)
    wh, wl = inverse(tab, p_oth, other, cross, p_cross, psq, share)
    all_res, wh = lax.optimization_barrier((all_res, wh))
    other_res = lax.ppermute(all_res, "c", swap)
    hi, lo, change = update_own(tab, wh, wl, all_res)
    out_t, step_share = update_other(hi, lo, other_res, change, res_t, share)
    return (out_t.T, step_share)


def solution(mesh):
    fine = Mesh(mesh.devices.reshape(4, 4, 2, 8, 2), EVERY)
    return jax.shard_map(
        on_device,
        mesh=fine,
        in_specs=(P(EVERY, None), P(EVERY, None), P()),
        out_specs=(P(EVERY, None), P(("zl", "c"), None)),
        check_vma=False,
    )
```
